128 devices in a mesh: wide: 32 (over x, y, core), narrow: 4 (over z).
Axes of the slice: x: 4, y: 4, z: 4, core: 2. Of those that a mesh axis runs over, the one named last changes fastest.
Arguments:
- phases: float32 [4, 1024, 128, 128], P(None, 'wide', 'narrow'), may hold values from 0 to 1
- potentials: float32 [2, 1024, 128, 128], P(None, 'wide', 'narrow'), may hold values from -1.5 to 1.5
- leaving: int32 [32, 4], P('wide', 'narrow'), may hold values from 0 to 3
- arriving: int32 [32, 4], P('wide', 'narrow'), may hold values from 0 to 31, as said below
- conc: float32 [4, 2], replicated, may hold values from -1 to 1
- latent: float32 [4], replicated, may hold values from -0.6 to 0.6
Outputs:
- phases_out: float32 [4, 1024, 128, 128], P(None, 'wide', 'narrow')
- potentials_out: float32 [2, 1024, 128, 128], P(None, 'wide', 'narrow')
The draws below stay inside these ranges and needn't reach their ends.
Inputs may be any that keep to these rules, and one draw needn't show every extreme that they name: In each block row, arriving is a permutation of the block columns, and each entry lies at most 2 columns away from its own column, cyclically; some entry lies exactly 2 away.
All inputs are finite; a program needn't handle non-finite values.
Results may differ from the reference program's by a relative error of at most 0.00012.
Values sent between devices are 32-bit elements; how exact they have to be, the bound alone decides.
A program may use at most 128 MiB of HBM per device.

```python
import jax
import jax.numpy as jnp

BLOCK = 32
SLOTS = 4
STEPS = 3
REACH = 2
BLOCK_COLS = 32
BLOCK_ROWS = 4
NX = 1024
NY = 128
NZ = 128


def lateral_parity():
    cols = jnp.arange(NX, dtype=jnp.int32) // BLOCK % 2
    rows = jnp.arange(NY, dtype=jnp.int32) // BLOCK % 2
    return (cols[:, None] + jnp.zeros((1, NY), jnp.int32), rows[None, :] + jnp.zeros((NX, 1), jnp.int32))


def draw_phases(key, part):
    key = jax.random.fold_in(key, 11)
    first = jax.random.fold_in(key, 0)
    cols, rows = lateral_parity()
    mixed = (cols + rows) % 2
    pattern = jnp.stack([mixed, cols, rows, 1 - mixed])
    level = jax.random.uniform(first, (4, NX, NY, NZ), jnp.float32)
    rough = 0.12 * level
    return jnp.where(pattern[..., None] == 1, 1.0 - rough, rough).astype(jnp.float32)


def draw_potentials(key, part):
    key = jax.random.fold_in(key, 13)
    first = jax.random.fold_in(key, 0)
    cols, rows = lateral_parity()
    signs = jnp.stack([1 - 2 * ((cols + rows) % 2), 1 - 2 * cols]).astype(jnp.float32)
    noise = jnp.clip(0.25 * jax.random.normal(first, (2, NX, NY, NZ), jnp.float32), -0.6, 0.6)
    offset = 0.9 * signs
    return (offset[..., None] + noise).astype(jnp.float32)


def draw_arriving(key, part):
    key = jax.random.fold_in(key, 7)
    first, second, third = jax.random.split(key, 3)
    shifts = jax.random.randint(first, (BLOCK_ROWS,), -REACH, REACH + 1)
    shifts = shifts.at[0].set(REACH)
    shifts = shifts.at[BLOCK_ROWS - 1].set(-REACH)
    paired = jax.random.randint(second, (BLOCK_ROWS,), 0, 2)
    use_swap = jnp.where(jnp.abs(shifts) < REACH, paired, 0)
    swaps = jax.random.randint(third, (BLOCK_ROWS, BLOCK_COLS // 2), 0, 2)
    columns = jnp.arange(BLOCK_COLS, dtype=jnp.int32)
    partner = jnp.bitwise_xor(columns, 1)
    flipped = jnp.take(swaps.T, columns // 2, axis=0) * use_swap[None, :]
    base = jnp.where(flipped == 1, partner[:, None], columns[:, None])
    return ((base - shifts[None, :]) % BLOCK_COLS).astype(jnp.int32)


def with_ends(entries, key, low, largest):
    dims = entries.shape
    place = [jax.random.randint(jax.random.fold_in(key, axis), (), 0, dims[axis]) for axis in range(len(dims))]
    entries = entries.at[tuple(place)].set(low)
    longest = dims.index(max(dims))
    place[longest] = (place[longest] + 1) % dims[longest]
    return entries.at[tuple(place)].set(largest)


def setup_inputs(seed: int = 0) -> dict:
    key_list = jax.random.split(jax.random.key(seed), 7)
    return {
        "phases": draw_phases(jax.random.fold_in(key_list[6], 71), 0),
        "potentials": draw_potentials(jax.random.fold_in(key_list[6], 71), 0),
        "leaving": with_ends(jax.random.randint(key_list[2], (BLOCK_COLS, BLOCK_ROWS), 0, SLOTS), jax.random.fold_in(key_list[2], 1), 0, SLOTS - 1).astype(jnp.int32),
        "arriving": draw_arriving(jax.random.fold_in(key_list[6], 71), 0),
        "conc": jnp.clip(jax.random.uniform(key_list[4], (4, 2), jnp.float32, -1.0, 1.0), -1.0, 1.0),
        "latent": jnp.clip(jax.random.uniform(key_list[5], (4,), jnp.float32, -0.6, 0.6), -0.6, 0.6),
    }


surface_weight = 1.0
drive_weight = 2.0
time_step = 0.1
diffusion = 1.0


def migrate(fields, leaving, arriving):
    comps = fields.shape[0]
    grid = fields.reshape(comps, BLOCK_COLS, BLOCK, BLOCK_ROWS, BLOCK, SLOTS, BLOCK)
    rowidx = jnp.arange(BLOCK_ROWS, dtype=jnp.int32)[None, :] + jnp.zeros((BLOCK_COLS, 1), jnp.int32)
    source_slot = leaving[arriving, rowidx]
    moved = grid[:, arriving, :, rowidx, :, source_slot, :]
    moved = jnp.transpose(moved, (2, 0, 3, 1, 4, 5))[:, :, :, :, :, None, :]
    slotidx = jnp.arange(SLOTS, dtype=jnp.int32)
    hit = leaving[:, :, None] == slotidx[None, None, :]
    hit = hit[None, :, None, :, None, :, None]
    grid = jnp.where(hit, moved, grid)
    return grid.reshape(fields.shape)


def laplace(field):
    xp = jnp.roll(field, -1, 1)
    xm = jnp.roll(field, 1, 1)
    yp = jnp.roll(field, -1, 2)
    ym = jnp.roll(field, 1, 2)
    zp = jnp.concatenate([field[..., 1:], field[..., -1:]], -1)
    zm = jnp.concatenate([field[..., :1], field[..., :-1]], -1)
    return xp + xm + yp + ym + zp + zm - 6.0 * field


def update(phase, potent, lap_phase, lap_potent, conc, latent, theta):
    well = phase * (1.0 - phase) * (1.0 - 2.0 * phase)
    slope = 6.0 * phase * (1.0 - phase)
    drive = conc[:, 0, None, None, None] * potent[0] + conc[:, 1, None, None, None] * potent[1] + latent[:, None, None, None] * theta
    rate = surface_weight * (lap_phase - 18.0 * well) - drive_weight * slope * drive
    rate = rate - jnp.mean(rate, axis=0, keepdims=True)
    new_phase = phase + time_step * rate
    change = new_phase - phase
    source = jnp.stack([jnp.sum(conc[:, 0, None, None, None] * change, 0), jnp.sum(conc[:, 1, None, None, None] * change, 0)])
    new_potent = potent + time_step * diffusion * lap_potent - source
    return new_phase, new_potent


def reference(phases, potentials, leaving, arriving, conc, latent):
    fields = migrate(jnp.concatenate([phases, potentials], 0), leaving, arriving)
    depth = fields.shape[3]
    theta = 4.0 * (jnp.arange(depth).astype(jnp.float32) + 0.5) / depth - 2.0
    phase = fields[:4]
    potent = fields[4:]
    for step in range(STEPS):
        phase, potent = update(phase, potent, laplace(phase), laplace(potent), conc, latent, theta)
    return phase, potent
```

```python
import functools

import jax
import jax.numpy as jnp
from jax import lax
from jax.experimental import pallas as pl
from jax.experimental.pallas import tpu as pltpu
from jax.sharding import PartitionSpec as P

MESH = pl.DeviceIdType.MESH
ROW0 = 12
ROWS = 56
PLANES = 38


def constants(latent):
    lane = lax.broadcasted_iota(jnp.int32, (8, 128), 1)
    theta = 4.0 * (lane.astype(jnp.float32) + 0.5) / 128.0 - 2.0
    base = [1.8 + (1.2 * latent[a]) * theta for a in range(4)]
    return lane == 0, lane == 127, base


def tile_step(get, conc, base, first, last):
    cen = [get(c, 0, 0) for c in range(6)]
    near = []
    for c in range(6):
        f = cen[c]
        zp = jnp.where(last, f, pltpu.roll(f, 127, 1))
        zm = jnp.where(first, f, pltpu.roll(f, 1, 1))
        near.append(
            ((get(c, 1, 0) + get(c, -1, 0)) + (get(c, 0, 1) + get(c, 0, -1))) + (zp + zm)
        )
    rate = []
    for a in range(4):
        p = cen[a]
        q = p - p * p
        e = (1.2 * conc[a, 0]) * cen[4] + (1.2 * conc[a, 1]) * cen[5] + (base[a] - 3.6 * p)
        rate.append((0.1 * near[a] - 0.6 * p) - q * e)
    mean = 0.25 * ((rate[0] + rate[1]) + (rate[2] + rate[3]))
    change = [r - mean for r in rate]
    out = [cen[a] + change[a] for a in range(4)]
    for k in range(2):
        source = (conc[0, k] * change[0] + conc[1, k] * change[1]) + (
            conc[2, k] * change[2] + conc[3, k] * change[3]
        )
        out.append((0.4 * cen[4 + k] + 0.1 * near[4 + k]) - source)
    return out


def kernel(
    leaving, arriving, conc, latent, phases, potentials, out_phases, out_potentials,
    A, B, C, OUT, PK, SIB, SR, SL, RR, RL, META, META_R, META_L,
    in_sem, out_sem, meta_send, meta_recv, sib_send, sib_recv,
    r_send, r_recv, l_send, l_recv, up_send, up_recv, dn_send, dn_recv, x_send, x_recv,
):
    w, n = lax.axis_index("wide"), lax.axis_index("narrow")
    columns, rows = lax.axis_size("wide"), lax.axis_size("narrow")
    core = w % 2
    chip = w // 2
    sib = w + 1 - 2 * core
    right, left = (w + 2) % columns, (w + columns - 2) % columns
    after, before = (w + 1) % columns, (w + columns - 1) % columns
    up, down = (n + 1) % rows, (n + rows - 1) % rows

    def piece_of(i):
        return (i + 7) % 8

    def inputs(p):
        x = pl.ds(4 * p, 4)
        to = pl.ds(4 * p + 3, 4)
        rr = pl.ds(ROW0, 32)
        return (
            pltpu.make_async_copy(phases.at[:, x], A.at[0:4, to, rr], in_sem.at[0, p]),
            pltpu.make_async_copy(potentials.at[:, x], A.at[4:6, to, rr], in_sem.at[1, p]),
        )

    @pl.loop(0, 8)
    def _(i):
        for copy in inputs(piece_of(i)):
            copy.start()

    barrier = pltpu.get_barrier_semaphore()
    for device in ((right, n), (left, n), (after, n), (before, n), (w, up), (w, down)):
        pl.semaphore_signal(barrier, inc=1, device_id=device, device_id_type=MESH)

    slot = leaving[0, 0]
    source = arriving[0, 0]
    META[...] = jnp.full((8, 128), source, jnp.int32)
    lane = lax.broadcasted_iota(jnp.int32, (8, 128), 1)
    group = lane // 32

    pl.semaphore_wait(barrier, 6)

    def remote(src, dst, send, recv, device):
        return pltpu.make_async_remote_copy(
            src_ref=src, dst_ref=dst, send_sem=send, recv_sem=recv,
            device_id=device, device_id_type=MESH,
        )

    metas = (
        remote(META, META_R, meta_send.at[0], meta_recv.at[0], (left, n)),
        remote(META, META_L, meta_send.at[1], meta_recv.at[1], (right, n)),
    )
    for copy in metas:
        copy.start()

    def to_sib(p):
        return remote(PK.at[p], SIB.at[p], sib_send.at[p], sib_recv.at[p], (sib, n))

    def to_right(p):
        return remote(SR.at[p], RL.at[p], r_send.at[p], r_recv.at[p], (right, n))

    def to_left(p):
        return remote(SL.at[p], RR.at[p], l_send.at[p], l_recv.at[p], (left, n))

    def to_up(h, x, count):
        xs = pl.ds(x, count)
        return remote(
            A.at[:, xs, pl.ds(ROW0 + 29, 3)], A.at[:, xs, pl.ds(ROW0 - 3, 3)],
            up_send.at[h], up_recv.at[h], (w, up),
        )

    def to_down(h, x, count):
        xs = pl.ds(x, count)
        return remote(
            A.at[:, xs, pl.ds(ROW0, 3)], A.at[:, xs, pl.ds(ROW0 + 32, 3)],
            dn_send.at[h], dn_recv.at[h], (w, down),
        )

    core_rows = pl.ds(ROW0, 32)
    to_after = remote(
        A.at[:, pl.ds(32, 3), core_rows], A.at[:, pl.ds(0, 3), core_rows],
        x_send.at[0], x_recv.at[0], (after, n),
    )
    to_before = remote(
        A.at[:, pl.ds(3, 3), core_rows], A.at[:, pl.ds(35, 3), core_rows],
        x_send.at[1], x_recv.at[1], (before, n),
    )

    def pack(i):
        p = piece_of(i)
        for copy in inputs(p):
            copy.wait()
        shifts = [(32 * g + 128 - 32 * slot) % 128 for g in range(4)]

        @pl.loop(0, 6)
        def _(c):
            for t in range(4):
                r = pl.ds(ROW0 + 8 * t, 8)
                v = [pltpu.roll(A[c, 4 * p + 3 + g, r, :], shifts[g], 1) for g in range(4)]
                low = jnp.where(group == 0, v[0], v[1])
                high = jnp.where(group == 2, v[2], v[3])
                PK[p, c, pl.ds(8 * t, 8), :] = jnp.where(group < 2, low, high)

        to_sib(p).start()

    def route(i):
        p = piece_of(i)
        to_sib(p).wait_recv()
        go_right = META_R[...] == sib
        go_left = META_L[...] == sib

        @pl.loop(0, 6)
        def _(c):
            for t in range(4):
                r = pl.ds(8 * t, 8)
                own, other = PK[p, c, r, :], SIB[p, c, r, :]
                SR[p, c, r, :] = jnp.where(go_right, other, own)
                SL[p, c, r, :] = jnp.where(go_left, other, own)

        to_right(p).start()
        to_left(p).start()

    from_col = jnp.full((8, 128), source, jnp.int32)
    from_own = from_col == w
    from_sib = from_col == sib
    left_col = (w - core + columns - 2) % columns
    from_left = (from_col == left_col) | (from_col == left_col + 1)
    target = group == jnp.full((8, 128), slot, jnp.int32)

    def merge(i):
        p = piece_of(i)
        to_right(p).wait_recv()
        to_left(p).wait_recv()
        shifts = [(128 + 32 * slot - 32 * g) % 128 for g in range(4)]

        @pl.loop(0, 6)
        def _(c):
            for t in range(4):
                r = pl.ds(8 * t, 8)
                v = jnp.where(from_left, RL[p, c, r, :], RR[p, c, r, :])
                v = jnp.where(from_sib, SIB[p, c, r, :], v)
                v = jnp.where(from_own, PK[p, c, r, :], v)
                for g in range(4):
                    x, rr = 4 * p + 3 + g, pl.ds(ROW0 + 8 * t, 8)
                    A[c, x, rr, :] = jnp.where(target, pltpu.roll(v, shifts[g], 1), A[c, x, rr, :])

        to_up(p, 4 * p + 3, 4).start()
        to_down(p, 4 * p + 3, 4).start()

    pl.loop(0, 2)(pack)
    for copy in metas:
        copy.wait_recv()

    @pl.loop(2, 8)
    def _(i):
        pack(i)
        route(i - 2)

    pl.loop(6, 8)(route)

    first, last, base = constants(latent)

    def sweep(src, dst, x0, x1, tiles, row0, plane_off, row_off):
        @pl.loop(x0, x1)
        def _(x):
            for t in range(tiles):
                i = row0 + 8 * t

                def get(c, dx, dy):
                    return src[c, x + dx, pl.ds(i + dy, 8), :]

                out = tile_step(get, conc, base, first, last)
                for c in range(6):
                    dst[c, x - plane_off, pl.ds(i - row_off, 8), :] = out[c]

    def outputs(h, x, count):
        xs = pl.ds(x, count)
        return (
            pltpu.make_async_copy(OUT.at[0:4, xs], out_phases.at[:, xs], out_sem.at[0, h]),
            pltpu.make_async_copy(OUT.at[4:6, xs], out_potentials.at[:, xs], out_sem.at[1, h]),
        )

    def steps(h, a0, a1, b0, b1, c0, c1, count):
        sweep(A, B, a0 + 3, a1 + 3, 5, 8, 0, 0)
        sweep(B, C, b0 + 3, b1 + 3, 5, 8, 0, 0)
        sweep(C, OUT, c0 + 3, c1 + 3, 4, ROW0, 3, ROW0)
        for copy in outputs(h, c0, count):
            copy.start()

    def halo_wait(h, x, count):
        to_up(h, x, count).wait_recv()
        to_down(h, x, count).wait_recv()

    merge(0)
    to_after.start()
    merge(1)
    to_before.start()
    merge(2)
    to_after.wait_recv()
    to_up(8, 0, 3).start()
    to_down(8, 0, 3).start()
    to_before.wait_recv()
    to_up(9, 35, 3).start()
    to_down(9, 35, 3).start()

    halo_wait(0, 3, 4)
    halo_wait(8, 0, 3)
    steps(0, -2, 3, -1, 2, 0, 1, 1)

    @pl.loop(3, 8)
    def _(i):
        merge(i)
        q = i - 2
        halo_wait(q, 4 * q + 3, 4)
        steps(q, 4 * q - 1, 4 * q + 3, 4 * q - 2, 4 * q + 2, 4 * q - 3, 4 * q + 1, 4)

    halo_wait(6, 27, 4)
    halo_wait(7, 31, 4)
    halo_wait(9, 35, 3)
    steps(6, 23, 34, 22, 33, 21, 32, 11)

    for copy in metas:
        copy.wait_send()
    to_after.wait_send()
    to_before.wait_send()

    @pl.loop(0, 8)
    def _(p):
        to_sib(p).wait_send()
        to_right(p).wait_send()
        to_left(p).wait_send()
        to_up(p, 4 * p + 3, 4).wait_send()
        to_down(p, 4 * p + 3, 4).wait_send()

    for h, x in ((8, 0), (9, 35)):
        to_up(h, x, 3).wait_send()
        to_down(h, x, 3).wait_send()
    for copy in outputs(0, 0, 1) + outputs(6, 21, 11):
        copy.wait()

    @pl.loop(1, 6)
    def _(q):
        for copy in outputs(q, 4 * q - 3, 4):
            copy.wait()


def shards(phases, potentials, leaving, arriving, conc, latent):
    f32, i32 = jnp.float32, jnp.int32
    smem = pl.BlockSpec(memory_space=pltpu.SMEM)
    hbm = pl.BlockSpec(memory_space=pl.ANY)
    ext = pltpu.VMEM((6, PLANES, ROWS, 128), f32)
    block = pltpu.VMEM((8, 6, 32, 128), f32)
    meta = pltpu.VMEM((8, 128), i32)
    dma = pltpu.SemaphoreType.DMA
    return tuple(
        pl.pallas_call(
            kernel,
            out_shape=(
                jax.ShapeDtypeStruct(phases.shape, f32),
                jax.ShapeDtypeStruct(potentials.shape, f32),
            ),
            in_specs=[smem] * 4 + [hbm] * 2,
            out_specs=(hbm, hbm),
            scratch_shapes=[
                ext, ext, ext, pltpu.VMEM((6, 32, 32, 128), f32),
                block, block, block, block, block, block, meta, meta, meta,
                dma((2, 8)), dma((2, 8)), dma((2,)), dma((2,)), dma((8,)), dma((8,)),
                dma((8,)), dma((8,)), dma((8,)), dma((8,)),
                dma((10,)), dma((10,)), dma((10,)), dma((10,)), dma((2,)), dma((2,)),
            ],
            compiler_params=pltpu.CompilerParams(
                collective_id=0, has_side_effects=True, vmem_limit_bytes=50 * 2**20
            ),
            cost_estimate=pl.CostEstimate(
                flops=60_000_000, bytes_accessed=6_400_000, transcendentals=0
            ),
        )(leaving, arriving, conc, latent, phases, potentials)
    )


def solution(mesh):
    field = P(None, "wide", "narrow", None)
    in_specs = (field, field, P("wide", "narrow"), P("wide", "narrow"), P(), P())
    return jax.shard_map(
        shards, mesh=mesh, in_specs=in_specs, out_specs=(field, field), check_vma=False
    )
```

```python
import functools

import jax
import jax.numpy as jnp
from jax import lax
from jax.experimental import pallas as pl
from jax.experimental.pallas import tpu as pltpu
from jax.sharding import PartitionSpec as P

MESH = pl.DeviceIdType.MESH
ROW0 = 12
ROWS = 56
PLANES = 38


def constants(conc, latent):
    lane = lax.broadcasted_iota(jnp.int32, (8, 128), 1)
    theta = 4.0 * (lane.astype(jnp.float32) + 0.5) / 128.0 - 2.0
    table = conc[...]
    weight = [
        [jnp.broadcast_to(table[k : k + 1, a : a + 1], (8, 128)) for k in range(2)]
        for a in range(4)
    ]
    pull = [[1.2 * weight[a][k] for k in range(2)] for a in range(4)]
    base = [1.8 + (1.2 * latent[0, a]) * theta for a in range(4)]
    return lane == 0, lane == 127, base, weight, pull


def tile_step(get, first, last, base, weight, pull):
    cen = [get(c, 0, 0) for c in range(6)]
    near = []
    for c in range(6):
        f = cen[c]
        zp = jnp.where(last, f, pltpu.roll(f, 127, 1))
        zm = jnp.where(first, f, pltpu.roll(f, 1, 1))
        near.append(
            ((get(c, 1, 0) + get(c, -1, 0)) + (get(c, 0, 1) + get(c, 0, -1))) + (zp + zm)
        )
    rate = []
    for a in range(4):
        p = cen[a]
        q = p - p * p
        e = pull[a][0] * cen[4] + pull[a][1] * cen[5] + (base[a] - 3.6 * p)
        rate.append((0.1 * near[a] - 0.6 * p) - q * e)
    mean = 0.25 * ((rate[0] + rate[1]) + (rate[2] + rate[3]))
    change = [r - mean for r in rate]
    out = [cen[a] + change[a] for a in range(4)]
    for k in range(2):
        source = (weight[0][k] * change[0] + weight[1][k] * change[1]) + (
            weight[2][k] * change[2] + weight[3][k] * change[3]
        )
        out.append((0.4 * cen[4 + k] + 0.1 * near[4 + k]) - source)
    return out


def kernel(
    leaving, arriving, conc, latent, phases, potentials, out_phases, out_potentials,
    A, B, C, CONC, PK, SIB, SR, SL, RR, RL, META, META_R, META_L,
    in_sem, conc_sem, meta_send, meta_recv, sib_send, sib_recv,
    r_send, r_recv, l_send, l_recv, up_send, up_recv, dn_send, dn_recv, x_send, x_recv,
):
    w, n = lax.axis_index("wide"), lax.axis_index("narrow")
    columns, rows = lax.axis_size("wide"), lax.axis_size("narrow")
    core = w % 2
    chip = w // 2
    sib = w + 1 - 2 * core
    right, left = (w + 2) % columns, (w + columns - 2) % columns
    after, before = (w + 1) % columns, (w + columns - 1) % columns
    up, down = (n + 1) % rows, (n + rows - 1) % rows

    def piece_of(i):
        return (i + 7) % 8

    def inputs(p):
        x = pl.ds(4 * p, 4)
        to = pl.ds(4 * p + 3, 4)
        rr = pl.ds(ROW0, 32)
        return (
            pltpu.make_async_copy(phases.at[:, x], A.at[0:4, to, rr], in_sem.at[0, p]),
            pltpu.make_async_copy(potentials.at[:, x], A.at[4:6, to, rr], in_sem.at[1, p]),
        )

    @pl.loop(0, 8)
    def _(i):
        for copy in inputs(piece_of(i)):
            copy.start()

    conc_copy = pltpu.make_async_copy(conc, CONC, conc_sem)
    conc_copy.start()
    barrier = pltpu.get_barrier_semaphore()
    for device in ((right, n), (left, n), (after, n), (before, n), (w, up), (w, down)):
        pl.semaphore_signal(barrier, inc=1, device_id=device, device_id_type=MESH)

    slot = leaving[0, 0]
    source = arriving[0, 0]
    META[...] = jnp.full((8, 128), source, jnp.int32)
    lane = lax.broadcasted_iota(jnp.int32, (8, 128), 1)
    group = lane // 32

    pl.semaphore_wait(barrier, 6)

    def remote(src, dst, send, recv, device):
        return pltpu.make_async_remote_copy(
            src_ref=src, dst_ref=dst, send_sem=send, recv_sem=recv,
            device_id=device, device_id_type=MESH,
        )

    metas = (
        remote(META, META_R, meta_send.at[0], meta_recv.at[0], (left, n)),
        remote(META, META_L, meta_send.at[1], meta_recv.at[1], (right, n)),
    )
    for copy in metas:
        copy.start()

    def to_sib(p):
        return remote(PK.at[p], SIB.at[p], sib_send.at[p], sib_recv.at[p], (sib, n))

    def to_right(p):
        return remote(SR.at[p], RL.at[p], r_send.at[p], r_recv.at[p], (right, n))

    def to_left(p):
        return remote(SL.at[p], RR.at[p], l_send.at[p], l_recv.at[p], (left, n))

    def to_up(h, x, count):
        xs = pl.ds(x, count)
        return remote(
            A.at[:, xs, pl.ds(ROW0 + 29, 3)], A.at[:, xs, pl.ds(ROW0 - 3, 3)],
            up_send.at[h], up_recv.at[h], (w, up),
        )

    def to_down(h, x, count):
        xs = pl.ds(x, count)
        return remote(
            A.at[:, xs, pl.ds(ROW0, 3)], A.at[:, xs, pl.ds(ROW0 + 32, 3)],
            dn_send.at[h], dn_recv.at[h], (w, down),
        )

    core_rows = pl.ds(ROW0, 32)
    to_after = remote(
        A.at[:, pl.ds(32, 3), core_rows], A.at[:, pl.ds(0, 3), core_rows],
        x_send.at[0], x_recv.at[0], (after, n),
    )
    to_before = remote(
        A.at[:, pl.ds(3, 3), core_rows], A.at[:, pl.ds(35, 3), core_rows],
        x_send.at[1], x_recv.at[1], (before, n),
    )

    def pack(i):
        p = piece_of(i)
        for copy in inputs(p):
            copy.wait()
        shifts = [(32 * g + 128 - 32 * slot) % 128 for g in range(4)]

        @pl.loop(0, 6)
        def _(c):
            for t in range(4):
                r = pl.ds(ROW0 + 8 * t, 8)
                v = [pltpu.roll(A[c, 4 * p + 3 + g, r, :], shifts[g], 1) for g in range(4)]
                low = jnp.where(group == 0, v[0], v[1])
                high = jnp.where(group == 2, v[2], v[3])
                PK[p, c, pl.ds(8 * t, 8), :] = jnp.where(group < 2, low, high)

        to_sib(p).start()

    def route(i):
        p = piece_of(i)
        to_sib(p).wait_recv()
        go_right = META_R[...] == sib
        go_left = META_L[...] == sib

        @pl.loop(0, 6)
        def _(c):
            for t in range(4):
                r = pl.ds(8 * t, 8)
                own, other = PK[p, c, r, :], SIB[p, c, r, :]
                SR[p, c, r, :] = jnp.where(go_right, other, own)
                SL[p, c, r, :] = jnp.where(go_left, other, own)

        to_right(p).start()
        to_left(p).start()

    from_col = jnp.full((8, 128), source, jnp.int32)
    from_own = from_col == w
    from_sib = from_col == sib
    left_col = (w - core + columns - 2) % columns
    from_left = (from_col == left_col) | (from_col == left_col + 1)
    target = group == jnp.full((8, 128), slot, jnp.int32)

    def merge(i):
        p = piece_of(i)
        to_right(p).wait_recv()
        to_left(p).wait_recv()
        shifts = [(128 + 32 * slot - 32 * g) % 128 for g in range(4)]

        @pl.loop(0, 6)
        def _(c):
            for t in range(4):
                r = pl.ds(8 * t, 8)
                v = jnp.where(from_left, RL[p, c, r, :], RR[p, c, r, :])
                v = jnp.where(from_sib, SIB[p, c, r, :], v)
                v = jnp.where(from_own, PK[p, c, r, :], v)
                for g in range(4):
                    x, rr = 4 * p + 3 + g, pl.ds(ROW0 + 8 * t, 8)
                    A[c, x, rr, :] = jnp.where(target, pltpu.roll(v, shifts[g], 1), A[c, x, rr, :])

        to_up(p, 4 * p + 3, 4).start()
        to_down(p, 4 * p + 3, 4).start()

    pl.loop(0, 2)(pack)
    for copy in metas:
        copy.wait_recv()

    @pl.loop(2, 5)
    def _(i):
        pack(i)
        route(i - 2)

    pl.loop(5, 8)(pack)
    conc_copy.wait()
    consts = constants(CONC, latent)

    def sweep(src, dst, x0, x1, tiles, row0):
        @pl.loop(x0, x1)
        def _(x):
            for t in range(tiles):
                i = row0 + 8 * t

                def get(c, dx, dy):
                    return src[c, x + dx, pl.ds(i + dy, 8), :]

                out = tile_step(get, *consts)
                for c in range(6):
                    dst[c, x, pl.ds(i, 8), :] = out[c]

    def steps(a0, a1, b0, b1, c0, c1):
        sweep(A, B, a0 + 3, a1 + 3, 5, 8)
        sweep(B, C, b0 + 3, b1 + 3, 5, 8)

        @pl.loop(c0, c1)
        def _(x):
            for t in range(4):
                i = ROW0 + 8 * t

                def get(c, dx, dy):
                    return C[c, x + 3 + dx, pl.ds(i + dy, 8), :]

                out = tile_step(get, *consts)
                for c in range(4):
                    out_phases[c, x, pl.ds(8 * t, 8), :] = out[c]
                for c in range(2):
                    out_potentials[c, x, pl.ds(8 * t, 8), :] = out[4 + c]

    def halo_wait(h, x, count):
        to_up(h, x, count).wait_recv()
        to_down(h, x, count).wait_recv()

    merge(0)
    to_after.start()
    route(3)
    merge(1)
    to_before.start()
    route(4)
    merge(2)
    route(5)
    halo_wait(0, 3, 4)

    @pl.loop(1, 6)
    def _(q):
        merge(q + 2)

        @pl.when(q < 3)
        def _():
            route(q + 5)

        @pl.when(q == 3)
        def _():
            to_after.wait_recv()
            to_up(8, 0, 3).start()
            to_down(8, 0, 3).start()
            to_before.wait_recv()
            to_up(9, 35, 3).start()
            to_down(9, 35, 3).start()

        halo_wait(q, 4 * q + 3, 4)
        cut = 1 - (q + 6) // 8
        steps(
            4 * q - 1, 4 * q + 3, 4 * q - 2 + 2 * cut, 4 * q + 2, 4 * q - 3 + 4 * cut, 4 * q + 1
        )

    halo_wait(8, 0, 3)
    steps(-2, 3, -1, 4, 0, 5)
    halo_wait(7, 31, 4)
    halo_wait(9, 35, 3)
    steps(29, 34, 30, 33, 31, 32)
    halo_wait(6, 27, 4)
    steps(23, 29, 22, 30, 21, 31)

    for copy in metas:
        copy.wait_send()
    to_after.wait_send()
    to_before.wait_send()

    @pl.loop(0, 8)
    def _(p):
        to_sib(p).wait_send()
        to_right(p).wait_send()
        to_left(p).wait_send()
        to_up(p, 4 * p + 3, 4).wait_send()
        to_down(p, 4 * p + 3, 4).wait_send()

    for h, x in ((8, 0), (9, 35)):
        to_up(h, x, 3).wait_send()
        to_down(h, x, 3).wait_send()


def store(phases, potentials, out_phases, out_potentials, sem):
    copies = [
        pltpu.make_async_copy(phases, out_phases, sem.at[0]),
        pltpu.make_async_copy(potentials, out_potentials, sem.at[1]),
    ]
    for copy in copies:
        copy.start()
    for copy in copies:
        copy.wait()


def shards(phases, potentials, leaving, arriving, conc, latent):
    f32, i32 = jnp.float32, jnp.int32
    smem = pl.BlockSpec(memory_space=pltpu.SMEM)
    hbm = pl.BlockSpec(memory_space=pltpu.HBM)
    vmem = pl.BlockSpec(memory_space=pltpu.VMEM)
    ext = pltpu.VMEM((6, PLANES, ROWS, 128), f32)
    block = pltpu.VMEM((8, 6, 32, 128), f32)
    meta = pltpu.VMEM((8, 128), i32)
    dma = pltpu.SemaphoreType.DMA
    shapes = (phases.shape, potentials.shape)
    results = pl.pallas_call(
        kernel,
        out_shape=tuple(pltpu.VMEM(s, f32) for s in shapes),
        in_specs=[smem, smem, hbm, smem, hbm, hbm],
        out_specs=(vmem, vmem),
        scratch_shapes=[
            ext, ext, ext, pltpu.VMEM((2, 4), f32),
            block, block, block, block, block, block, meta, meta, meta,
            dma((2, 8)), dma, dma((2,)), dma((2,)), dma((8,)), dma((8,)),
            dma((8,)), dma((8,)), dma((8,)), dma((8,)),
            dma((10,)), dma((10,)), dma((10,)), dma((10,)), dma((2,)), dma((2,)),
        ],
        compiler_params=pltpu.CompilerParams(
            collective_id=0, has_side_effects=True, vmem_limit_bytes=60 * 2**20
        ),
        cost_estimate=pl.CostEstimate(
            flops=60_000_000, bytes_accessed=6_400_000, transcendentals=0
        ),
    )(leaving, arriving, conc.T, latent.reshape(1, 4), phases, potentials)
    return tuple(
        pl.pallas_call(
            store,
            out_shape=tuple(jax.ShapeDtypeStruct(s, f32) for s in shapes),
            in_specs=[vmem, vmem],
            compiler_params=pltpu.CompilerParams(vmem_limit_bytes=2**18),
            out_specs=(hbm, hbm),
            scratch_shapes=[dma((2,))],
        )(*results)
    )


def solution(mesh):
    field = P(None, "wide", "narrow", None)
    in_specs = (field, field, P("wide", "narrow"), P("wide", "narrow"), P(), P())
    return jax.shard_map(
        shards, mesh=mesh, in_specs=in_specs, out_specs=(field, field), check_vma=False
    )
```

```python
import functools

import jax
import jax.numpy as jnp
from jax import lax
from jax.experimental import pallas as pl
from jax.experimental.pallas import tpu as pltpu
from jax.sharding import PartitionSpec as P

MESH = pl.DeviceIdType.MESH
ROW0 = 12
ROWS = 56
PLANES = 38


MXU = 4


def neighbour_matrix():
    row = lax.broadcasted_iota(jnp.int32, (256, 128), 0) % 128
    col = lax.broadcasted_iota(jnp.int32, (256, 128), 1)
    edge = (row == col) & ((row == 0) | (row == 127))
    near = (row - col == 1) | (col - row == 1) | edge
    return near.astype(jnp.float32).astype(jnp.bfloat16)


def constants(conc, latent):
    lane = lax.broadcasted_iota(jnp.int32, (8, 128), 1)
    theta = 4.0 * (lane.astype(jnp.float32) + 0.5) / 128.0 - 2.0
    table = conc[...]
    weight = [
        [jnp.broadcast_to(table[k : k + 1, a : a + 1], (8, 128)) for k in range(2)]
        for a in range(4)
    ]
    pull = [[1.2 * weight[a][k] for k in range(2)] for a in range(4)]
    base = [1.8 + (1.2 * latent[0, a]) * theta for a in range(4)]
    return lane == 0, lane == 127, base, weight, pull


def tile_step(get, along, first, last, base, weight, pull):
    cen = [get(c, 0, 0) for c in range(6)]
    near = []
    for c in range(6):
        f = cen[c]
        if c < MXU:
            z = along(c)
        else:
            zp = jnp.where(last, f, pltpu.roll(f, 127, 1))
            zm = jnp.where(first, f, pltpu.roll(f, 1, 1))
            z = zp + zm
        near.append(((get(c, 1, 0) + get(c, -1, 0)) + (get(c, 0, 1) + get(c, 0, -1))) + z)
    rate = []
    for a in range(4):
        p = cen[a]
        q = p - p * p
        e = pull[a][0] * cen[4] + pull[a][1] * cen[5] + (base[a] - 3.6 * p)
        rate.append((0.1 * near[a] - 0.6 * p) - q * e)
    mean = 0.25 * ((rate[0] + rate[1]) + (rate[2] + rate[3]))
    change = [r - mean for r in rate]
    out = [cen[a] + change[a] for a in range(4)]
    for k in range(2):
        source = (weight[0][k] * change[0] + weight[1][k] * change[1]) + (
            weight[2][k] * change[2] + weight[3][k] * change[3]
        )
        out.append((0.4 * cen[4 + k] + 0.1 * near[4 + k]) - source)
    return out


def kernel(
    leaving, arriving, conc, latent, phases, potentials, out_phases, out_potentials,
    A, B, C, NEAR, CONC, PK, SIB, SR, SL, RR, RL, META, META_R, META_L,
    in_sem, conc_sem, meta_send, meta_recv, sib_send, sib_recv,
    r_send, r_recv, l_send, l_recv, up_send, up_recv, dn_send, dn_recv, x_send, x_recv,
):
    w, n = lax.axis_index("wide"), lax.axis_index("narrow")
    columns, rows = lax.axis_size("wide"), lax.axis_size("narrow")
    core = w % 2
    chip = w // 2
    sib = w + 1 - 2 * core
    right, left = (w + 2) % columns, (w + columns - 2) % columns
    after, before = (w + 1) % columns, (w + columns - 1) % columns
    up, down = (n + 1) % rows, (n + rows - 1) % rows

    def piece_of(i):
        return (i + 7) % 8

    def inputs(p):
        x = pl.ds(4 * p, 4)
        to = pl.ds(4 * p + 3, 4)
        rr = pl.ds(ROW0, 32)
        return (
            pltpu.make_async_copy(phases.at[:, x], A.at[0:4, to, rr], in_sem.at[0, p]),
            pltpu.make_async_copy(potentials.at[:, x], A.at[4:6, to, rr], in_sem.at[1, p]),
        )

    @pl.loop(0, 8)
    def _(i):
        for copy in inputs(piece_of(i)):
            copy.start()

    conc_copy = pltpu.make_async_copy(conc, CONC, conc_sem)
    conc_copy.start()
    barrier = pltpu.get_barrier_semaphore()
    for device in ((right, n), (left, n), (after, n), (before, n), (w, up), (w, down)):
        pl.semaphore_signal(barrier, inc=1, device_id=device, device_id_type=MESH)

    NEAR[...] = neighbour_matrix()
    slot = leaving[0, 0]
    source = arriving[0, 0]
    META[...] = jnp.full((8, 128), source, jnp.int32)
    lane = lax.broadcasted_iota(jnp.int32, (8, 128), 1)
    group = lane // 32

    pl.semaphore_wait(barrier, 6)

    def remote(src, dst, send, recv, device):
        return pltpu.make_async_remote_copy(
            src_ref=src, dst_ref=dst, send_sem=send, recv_sem=recv,
            device_id=device, device_id_type=MESH,
        )

    metas = (
        remote(META, META_R, meta_send.at[0], meta_recv.at[0], (left, n)),
        remote(META, META_L, meta_send.at[1], meta_recv.at[1], (right, n)),
    )
    for copy in metas:
        copy.start()

    def to_sib(p):
        return remote(PK.at[p], SIB.at[p], sib_send.at[p], sib_recv.at[p], (sib, n))

    def to_right(p):
        return remote(SR.at[p], RL.at[p], r_send.at[p], r_recv.at[p], (right, n))

    def to_left(p):
        return remote(SL.at[p], RR.at[p], l_send.at[p], l_recv.at[p], (left, n))

    def to_up(h, x, count):
        xs = pl.ds(x, count)
        return remote(
            A.at[:, xs, pl.ds(ROW0 + 29, 3)], A.at[:, xs, pl.ds(ROW0 - 3, 3)],
            up_send.at[h], up_recv.at[h], (w, up),
        )

    def to_down(h, x, count):
        xs = pl.ds(x, count)
        return remote(
            A.at[:, xs, pl.ds(ROW0, 3)], A.at[:, xs, pl.ds(ROW0 + 32, 3)],
            dn_send.at[h], dn_recv.at[h], (w, down),
        )

    core_rows = pl.ds(ROW0, 32)
    to_after = remote(
        A.at[:, pl.ds(32, 3), core_rows], A.at[:, pl.ds(0, 3), core_rows],
        x_send.at[0], x_recv.at[0], (after, n),
    )
    to_before = remote(
        A.at[:, pl.ds(3, 3), core_rows], A.at[:, pl.ds(35, 3), core_rows],
        x_send.at[1], x_recv.at[1], (before, n),
    )

    def pack(i):
        p = piece_of(i)
        for copy in inputs(p):
            copy.wait()
        shifts = [(32 * g + 128 - 32 * slot) % 128 for g in range(4)]

        @pl.loop(0, 6)
        def _(c):
            for t in range(4):
                r = pl.ds(ROW0 + 8 * t, 8)
                v = [pltpu.roll(A[c, 4 * p + 3 + g, r, :], shifts[g], 1) for g in range(4)]
                low = jnp.where(group == 0, v[0], v[1])
                high = jnp.where(group == 2, v[2], v[3])
                PK[p, c, pl.ds(8 * t, 8), :] = jnp.where(group < 2, low, high)

        to_sib(p).start()

    def route(i):
        p = piece_of(i)
        to_sib(p).wait_recv()
        go_right = META_R[...] == sib
        go_left = META_L[...] == sib

        @pl.loop(0, 6)
        def _(c):
            for t in range(4):
                r = pl.ds(8 * t, 8)
                own, other = PK[p, c, r, :], SIB[p, c, r, :]
                SR[p, c, r, :] = jnp.where(go_right, other, own)
                SL[p, c, r, :] = jnp.where(go_left, other, own)

        to_right(p).start()
        to_left(p).start()

    from_col = jnp.full((8, 128), source, jnp.int32)
    from_own = from_col == w
    from_sib = from_col == sib
    left_col = (w - core + columns - 2) % columns
    from_left = (from_col == left_col) | (from_col == left_col + 1)
    target = group == jnp.full((8, 128), slot, jnp.int32)

    def merge(i):
        p = piece_of(i)
        to_right(p).wait_recv()
        to_left(p).wait_recv()
        shifts = [(128 + 32 * slot - 32 * g) % 128 for g in range(4)]

        @pl.loop(0, 6)
        def _(c):
            for t in range(4):
                r = pl.ds(8 * t, 8)
                v = jnp.where(from_left, RL[p, c, r, :], RR[p, c, r, :])
                v = jnp.where(from_sib, SIB[p, c, r, :], v)
                v = jnp.where(from_own, PK[p, c, r, :], v)
                for g in range(4):
                    x, rr = 4 * p + 3 + g, pl.ds(ROW0 + 8 * t, 8)
                    A[c, x, rr, :] = jnp.where(target, pltpu.roll(v, shifts[g], 1), A[c, x, rr, :])

        to_up(p, 4 * p + 3, 4).start()
        to_down(p, 4 * p + 3, 4).start()

    pl.loop(0, 2)(pack)
    for copy in metas:
        copy.wait_recv()

    @pl.loop(2, 5)
    def _(i):
        pack(i)
        route(i - 2)

    pl.loop(5, 8)(pack)
    conc_copy.wait()
    consts = constants(CONC, latent)

    def update(src, store, x0, planes, tiles, row0):
        rows = 8 * tiles
        f = jnp.concatenate(
            [src[c, x0 + k, pl.ds(row0, rows), :] for k in range(planes) for c in range(MXU)], 0
        )
        high = f.astype(jnp.bfloat16)
        low = (f - high.astype(jnp.float32)).astype(jnp.bfloat16)
        sums = jnp.dot(
            jnp.concatenate([high, low], 1), NEAR[...], preferred_element_type=jnp.float32
        )
        for k in range(planes):
            x = x0 + k
            for t in range(tiles):
                i = row0 + 8 * t

                def get(c, dx, dy):
                    return src[c, x + dx, pl.ds(i + dy, 8), :]

                def along(c):
                    at = (k * MXU + c) * rows + 8 * t
                    return sums[at : at + 8]

                store(x, i, tile_step(get, along, *consts))

    def into(dst):
        def store(x, i, out):
            for c in range(6):
                dst[c, x, pl.ds(i, 8), :] = out[c]

        return store

    def result(x, i, out):
        for c in range(4):
            out_phases[c, x - 3, pl.ds(i - ROW0, 8), :] = out[c]
        for c in range(2):
            out_potentials[c, x - 3, pl.ds(i - ROW0, 8), :] = out[4 + c]

    def chunked(src, store, x0, planes, tiles, row0):
        size = planes if planes <= 6 else planes // 2
        if size == planes:
            update(src, store, x0, size, tiles, row0)
        else:
            @pl.loop(0, planes // size)
            def _(j):
                update(src, store, x0 + size * j, size, tiles, row0)

    def steps(a, na, b, nb, c, nc):
        chunked(A, into(B), a + 3, na, 5, 8)
        chunked(B, into(C), b + 3, nb, 5, 8)
        chunked(C, result, c + 3, nc, 4, ROW0)

    def halo_wait(h, x, count):
        to_up(h, x, count).wait_recv()
        to_down(h, x, count).wait_recv()

    merge(0)
    to_after.start()
    route(3)
    merge(1)
    to_before.start()
    route(4)
    merge(2)
    route(5)
    halo_wait(0, 3, 4)

    merge(3)
    route(6)
    halo_wait(1, 7, 4)
    steps(1, 6, 2, 4, 3, 2)

    @pl.loop(2, 6)
    def _(q):
        merge(q + 2)

        @pl.when(q == 2)
        def _():
            route(7)

        @pl.when(q == 3)
        def _():
            to_after.wait_recv()
            to_up(8, 0, 3).start()
            to_down(8, 0, 3).start()
            to_before.wait_recv()
            to_up(9, 35, 3).start()
            to_down(9, 35, 3).start()

        halo_wait(q, 4 * q + 3, 4)
        steps(4 * q - 1, 4, 4 * q - 2, 4, 4 * q - 3, 4)

    halo_wait(8, 0, 3)
    steps(-2, 3, -1, 3, 0, 3)
    halo_wait(7, 31, 4)
    halo_wait(9, 35, 3)
    steps(29, 5, 30, 3, 31, 1)
    halo_wait(6, 27, 4)
    steps(23, 6, 22, 8, 21, 10)

    for copy in metas:
        copy.wait_send()
    to_after.wait_send()
    to_before.wait_send()

    @pl.loop(0, 8)
    def _(p):
        to_sib(p).wait_send()
        to_right(p).wait_send()
        to_left(p).wait_send()
        to_up(p, 4 * p + 3, 4).wait_send()
        to_down(p, 4 * p + 3, 4).wait_send()

    for h, x in ((8, 0), (9, 35)):
        to_up(h, x, 3).wait_send()
        to_down(h, x, 3).wait_send()


def store(phases, potentials, out_phases, out_potentials, sem):
    copies = [
        pltpu.make_async_copy(phases, out_phases, sem.at[0]),
        pltpu.make_async_copy(potentials, out_potentials, sem.at[1]),
    ]
    for copy in copies:
        copy.start()
    for copy in copies:
        copy.wait()


def shards(phases, potentials, leaving, arriving, conc, latent):
    f32, i32 = jnp.float32, jnp.int32
    smem = pl.BlockSpec(memory_space=pltpu.SMEM)
    hbm = pl.BlockSpec(memory_space=pltpu.HBM)
    vmem = pl.BlockSpec(memory_space=pltpu.VMEM)
    ext = pltpu.VMEM((6, PLANES, ROWS, 128), f32)
    block = pltpu.VMEM((8, 6, 32, 128), f32)
    meta = pltpu.VMEM((8, 128), i32)
    dma = pltpu.SemaphoreType.DMA
    shapes = (phases.shape, potentials.shape)
    results = pl.pallas_call(
        kernel,
        out_shape=tuple(pltpu.VMEM(s, f32) for s in shapes),
        in_specs=[smem, smem, hbm, smem, hbm, hbm],
        out_specs=(vmem, vmem),
        scratch_shapes=[
            ext, ext, ext, pltpu.VMEM((256, 128), jnp.bfloat16), pltpu.VMEM((2, 4), f32),
            block, block, block, block, block, block, meta, meta, meta,
            dma((2, 8)), dma, dma((2,)), dma((2,)), dma((8,)), dma((8,)),
            dma((8,)), dma((8,)), dma((8,)), dma((8,)),
            dma((10,)), dma((10,)), dma((10,)), dma((10,)), dma((2,)), dma((2,)),
        ],
        compiler_params=pltpu.CompilerParams(
            collective_id=0, has_side_effects=True, vmem_limit_bytes=60 * 2**20
        ),
        cost_estimate=pl.CostEstimate(
            flops=60_000_000, bytes_accessed=6_400_000, transcendentals=0
        ),
    )(leaving, arriving, conc.T, latent.reshape(1, 4), phases, potentials)
    return tuple(
        pl.pallas_call(
            store,
            out_shape=tuple(jax.ShapeDtypeStruct(s, f32) for s in shapes),
            in_specs=[vmem, vmem],
            compiler_params=pltpu.CompilerParams(vmem_limit_bytes=2**18),
            out_specs=(hbm, hbm),
            scratch_shapes=[dma((2,))],
        )(*results)
    )


def solution(mesh):
    field = P(None, "wide", "narrow", None)
    in_specs = (field, field, P("wide", "narrow"), P("wide", "narrow"), P(), P())
    return jax.shard_map(
        shards, mesh=mesh, in_specs=in_specs, out_specs=(field, field), check_vma=False
    )
```

```python
import functools

import jax
import jax.numpy as jnp
from jax import lax
from jax.experimental import pallas as pl
from jax.experimental.pallas import tpu as pltpu
from jax.sharding import PartitionSpec as P

MESH = pl.DeviceIdType.MESH
ROW0 = 12
ROWS = 56
PLANES = 38


MXU = 4


EARLY = ((7, 0), (7, 1), (0, 0), (0, 1), (1, 0), (2, 0), (3, 0), (1, 1))
LATE = ((4, 0), (2, 1), (5, 0), (3, 1), (6, 0), (4, 1), (5, 1), (6, 1))


def neighbour_matrix():
    row = lax.broadcasted_iota(jnp.int32, (256, 128), 0) % 128
    col = lax.broadcasted_iota(jnp.int32, (256, 128), 1)
    edge = (row == col) & ((row == 0) | (row == 127))
    near = (row - col == 1) | (col - row == 1) | edge
    return near.astype(jnp.float32).astype(jnp.bfloat16)


def constants(conc, latent):
    lane = lax.broadcasted_iota(jnp.int32, (8, 128), 1)
    theta = 4.0 * (lane.astype(jnp.float32) + 0.5) / 128.0 - 2.0
    table = conc[...]
    weight = [
        [jnp.broadcast_to(table[k : k + 1, a : a + 1], (8, 128)) for k in range(2)]
        for a in range(4)
    ]
    pull = [[1.2 * weight[a][k] for k in range(2)] for a in range(4)]
    base = [1.8 + (1.2 * latent[0, a]) * theta for a in range(4)]
    return lane == 0, lane == 127, base, weight, pull


def tile_step(get, along, first, last, base, weight, pull):
    cen = [get(c, 0, 0) for c in range(6)]
    near = []
    for c in range(6):
        f = cen[c]
        if c < MXU:
            z = along(c)
        else:
            zp = jnp.where(last, f, pltpu.roll(f, 127, 1))
            zm = jnp.where(first, f, pltpu.roll(f, 1, 1))
            z = zp + zm
        near.append(((get(c, 1, 0) + get(c, -1, 0)) + (get(c, 0, 1) + get(c, 0, -1))) + z)
    rate = []
    for a in range(4):
        p = cen[a]
        q = p - p * p
        e = pull[a][0] * cen[4] + pull[a][1] * cen[5] + (base[a] - 3.6 * p)
        rate.append((0.1 * near[a] - 0.6 * p) - q * e)
    mean = 0.25 * ((rate[0] + rate[1]) + (rate[2] + rate[3]))
    change = [r - mean for r in rate]
    out = [cen[a] + change[a] for a in range(4)]
    for k in range(2):
        source = (weight[0][k] * change[0] + weight[1][k] * change[1]) + (
            weight[2][k] * change[2] + weight[3][k] * change[3]
        )
        out.append((0.4 * cen[4 + k] + 0.1 * near[4 + k]) - source)
    return out


def kernel(
    leaving_in, arriving_in, conc, latent, phases, potentials, out_phases, out_potentials,
    A, B, C, NEAR, CONC, leaving, arriving, PK, TO_SIB, SIB, SR, SL, RR, RL, META, META_SIB, META_R, META_L,
    in_sem, small_sem, meta_send, meta_recv, sib_send, sib_recv,
    r_send, r_recv, l_send, l_recv, up_send, up_recv, dn_send, dn_recv, x_send, x_recv,
):
    w, n = lax.axis_index("wide"), lax.axis_index("narrow")
    columns, rows = lax.axis_size("wide"), lax.axis_size("narrow")
    core = w % 2
    chip = w // 2
    sib = w + 1 - 2 * core
    right, left = (w + 2) % columns, (w + columns - 2) % columns
    after, before = (w + 1) % columns, (w + columns - 1) % columns
    up, down = (n + 1) % rows, (n + rows - 1) % rows

    def inputs(p):
        x = pl.ds(4 * p, 4)
        to = pl.ds(4 * p + 3, 4)
        rr = pl.ds(ROW0, 32)
        return (
            pltpu.make_async_copy(phases.at[:, x], A.at[0:4, to, rr], in_sem.at[0, p]),
            pltpu.make_async_copy(potentials.at[:, x], A.at[4:6, to, rr], in_sem.at[1, p]),
        )

    @pl.loop(0, 8)
    def _(i):
        for copy in inputs((i + 7) % 8):
            copy.start()

    small = [
        pltpu.make_async_copy(src, dst, small_sem.at[i])
        for i, (src, dst) in enumerate(
            ((leaving_in, leaving), (arriving_in, arriving), (conc, CONC))
        )
    ]
    for copy in small:
        copy.start()
    barrier = pltpu.get_barrier_semaphore()
    for device in ((right, n), (left, n), (after, n), (before, n), (w, up), (w, down)):
        pl.semaphore_signal(barrier, inc=1, device_id=device, device_id_type=MESH)

    NEAR[...] = neighbour_matrix()
    for copy in small:
        copy.wait()
    slot = leaving[0, 0]
    source = arriving[0, 0]
    META[...] = jnp.full((8, 128), source, jnp.int32)
    lane = lax.broadcasted_iota(jnp.int32, (8, 128), 1)
    group = lane // 32

    def remote(src, dst, send, recv, device):
        return pltpu.make_async_remote_copy(
            src_ref=src, dst_ref=dst, send_sem=send, recv_sem=recv,
            device_id=device, device_id_type=MESH,
        )

    metas = (
        remote(META, META_SIB, meta_send.at[0], meta_recv.at[0], (sib, n)),
        remote(META, META_R, meta_send.at[1], meta_recv.at[1], (left, n)),
        remote(META, META_L, meta_send.at[2], meta_recv.at[2], (right, n)),
    )

    def to_sib(p, h):
        src = TO_SIB if (p, h) in EARLY else PK
        return remote(src.at[p, h], SIB.at[p, h], sib_send.at[p, h], sib_recv.at[p, h], (sib, n))

    def to_right(p, h):
        src = PK if (p, h) in EARLY else SR
        return remote(src.at[p, h], RL.at[p, h], r_send.at[p, h], r_recv.at[p, h], (right, n))

    def to_left(p, h):
        src = PK if (p, h) in EARLY else SL
        return remote(src.at[p, h], RR.at[p, h], l_send.at[p, h], l_recv.at[p, h], (left, n))

    def to_up(h, x, count):
        xs = pl.ds(x, count)
        return remote(
            A.at[:, xs, pl.ds(ROW0 + 29, 3)], A.at[:, xs, pl.ds(ROW0 - 3, 3)],
            up_send.at[h], up_recv.at[h], (w, up),
        )

    def to_down(h, x, count):
        xs = pl.ds(x, count)
        return remote(
            A.at[:, xs, pl.ds(ROW0, 3)], A.at[:, xs, pl.ds(ROW0 + 32, 3)],
            dn_send.at[h], dn_recv.at[h], (w, down),
        )

    core_rows = pl.ds(ROW0, 32)
    to_after = remote(
        A.at[:, pl.ds(32, 3), core_rows], A.at[:, pl.ds(0, 3), core_rows],
        x_send.at[0], x_recv.at[0], (after, n),
    )
    to_before = remote(
        A.at[:, pl.ds(3, 3), core_rows], A.at[:, pl.ds(35, 3), core_rows],
        x_send.at[1], x_recv.at[1], (before, n),
    )

    tiles_of = ((0, 3), (1, 2))

    def pack(p):
        for copy in inputs(p):
            copy.wait()
        shifts = [(32 * g + 128 - 32 * slot) % 128 for g in range(4)]

        for c in range(6):
            for h in range(2):
                for k, t in enumerate(tiles_of[h]):
                    r = pl.ds(ROW0 + 8 * t, 8)
                    v = [pltpu.roll(A[c, 4 * p + 3 + g, r, :], shifts[g], 1) for g in range(4)]
                    low = jnp.where(group == 0, v[0], v[1])
                    high = jnp.where(group == 2, v[2], v[3])
                    PK[p, h, c, pl.ds(8 * k, 8), :] = jnp.where(group < 2, low, high)

    def send(p, h):
        to_right(p, h).start()
        to_left(p, h).start()

    from_col = jnp.full((8, 128), source, jnp.int32)
    from_own, from_left, from_right = from_col == w, from_col == left, from_col == right
    from_sib = from_col == sib
    from_left_chip = from_left | (from_col == (sib + columns - 2) % columns)
    target = group == jnp.full((8, 128), slot, jnp.int32)

    def forward(p, h):
        to_right(p, h).wait_recv()
        to_left(p, h).wait_recv()
        want = META_SIB[...]
        own, from_l = want == w, want == left

        for c in range(6):
            for k in range(2):
                r = pl.ds(8 * k, 8)
                v = jnp.where(from_l, RL[p, h, c, r, :], RR[p, h, c, r, :])
                TO_SIB[p, h, c, r, :] = jnp.where(own, PK[p, h, c, r, :], v)

        to_sib(p, h).start()

    def route(p, h):
        to_sib(p, h).wait_recv()
        go_right, go_left = META_R[...] == sib, META_L[...] == sib
        for c in range(6):
            for k in range(2):
                r = pl.ds(8 * k, 8)
                own, other = PK[p, h, c, r, :], SIB[p, h, c, r, :]
                SR[p, h, c, r, :] = jnp.where(go_right, other, own)
                SL[p, h, c, r, :] = jnp.where(go_left, other, own)
        send(p, h)

    def merge(p, h):
        if (p, h) in EARLY:
            to_sib(p, h).wait_recv()
        else:
            to_right(p, h).wait_recv()
            to_left(p, h).wait_recv()
        shifts = [(128 + 32 * slot - 32 * g) % 128 for g in range(4)]

        for c in range(6):
            for k, t in enumerate(tiles_of[h]):
                r = pl.ds(8 * k, 8)
                if (p, h) in EARLY:
                    v = jnp.where(from_left, RL[p, h, c, r, :], SIB[p, h, c, r, :])
                    v = jnp.where(from_right, RR[p, h, c, r, :], v)
                else:
                    v = jnp.where(from_left_chip, RL[p, h, c, r, :], RR[p, h, c, r, :])
                    v = jnp.where(from_sib, SIB[p, h, c, r, :], v)
                v = jnp.where(from_own, PK[p, h, c, r, :], v)
                for g in range(4):
                    x, rr = 4 * p + 3 + g, pl.ds(ROW0 + 8 * t, 8)
                    A[c, x, rr, :] = jnp.where(target, pltpu.roll(v, shifts[g], 1), A[c, x, rr, :])

        if h == 0:
            to_up(p, 4 * p + 3, 4).start()
            to_down(p, 4 * p + 3, 4).start()

    pack(7)
    pl.semaphore_wait(barrier, 6)
    send(7, 0)
    send(7, 1)
    for copy in metas:
        copy.start()
    pack(0)
    send(0, 0)
    send(0, 1)
    pack(1)
    send(1, 0)
    pack(2)
    send(2, 0)
    pack(3)
    send(3, 0)
    send(1, 1)
    pl.loop(4, 7)(pack)
    for p, h in LATE:
        to_sib(p, h).start()
    for copy in metas:
        copy.wait_recv()

    consts = constants(CONC, latent)

    def update(src, store, x0, planes, tiles, row0):
        rows = 8 * tiles
        f = jnp.concatenate(
            [src[c, x0 + k, pl.ds(row0, rows), :] for k in range(planes) for c in range(MXU)], 0
        )
        high = f.astype(jnp.bfloat16)
        low = (f - high.astype(jnp.float32)).astype(jnp.bfloat16)
        sums = jnp.dot(
            jnp.concatenate([high, low], 1), NEAR[...], preferred_element_type=jnp.float32
        )
        for k in range(planes):
            x = x0 + k
            for t in range(tiles):
                i = row0 + 8 * t

                def get(c, dx, dy):
                    return src[c, x + dx, pl.ds(i + dy, 8), :]

                def along(c):
                    at = (k * MXU + c) * rows + 8 * t
                    return sums[at : at + 8]

                store(x, i, tile_step(get, along, *consts))

    def into(dst):
        def store(x, i, out):
            for c in range(6):
                dst[c, x, pl.ds(i, 8), :] = out[c]

        return store

    def result(x, i, out):
        for c in range(4):
            out_phases[c, x - 3, pl.ds(i - ROW0, 8), :] = out[c]
        for c in range(2):
            out_potentials[c, x - 3, pl.ds(i - ROW0, 8), :] = out[4 + c]

    def chunked(src, store, x0, planes, tiles, row0):
        size = planes if planes <= 6 else planes // 2
        if size == planes:
            update(src, store, x0, size, tiles, row0)
        else:
            @pl.loop(0, planes // size)
            def _(j):
                update(src, store, x0 + size * j, size, tiles, row0)

    def steps(a, na, b, nb, c, nc):
        chunked(A, into(B), a + 3, na, 5, 8)
        chunked(B, into(C), b + 3, nb, 5, 8)
        chunked(C, result, c + 3, nc, 4, ROW0)

    def halo_wait(h, x, count):
        to_up(h, x, count).wait_recv()
        to_down(h, x, count).wait_recv()

    forward(7, 0)
    forward(7, 1)
    forward(0, 0)
    merge(7, 0)
    merge(7, 1)
    to_after.start()
    forward(0, 1)
    merge(0, 0)
    forward(1, 0)
    merge(0, 1)
    to_before.start()
    for p, h in LATE:
        route(p, h)
    merge(1, 0)
    forward(2, 0)
    forward(3, 0)
    merge(2, 0)
    forward(1, 1)
    merge(3, 0)
    merge(1, 1)
    halo_wait(0, 3, 4)
    halo_wait(1, 7, 4)
    steps(1, 6, 2, 4, 3, 2)
    to_after.wait_recv()
    to_up(8, 0, 3).start()
    to_down(8, 0, 3).start()
    to_before.wait_recv()
    to_up(9, 35, 3).start()
    to_down(9, 35, 3).start()
    merge(4, 0)
    merge(2, 1)
    halo_wait(8, 0, 3)
    steps(-2, 3, -1, 3, 0, 3)
    halo_wait(7, 31, 4)
    halo_wait(9, 35, 3)
    steps(29, 5, 30, 3, 31, 1)

    @pl.loop(2, 6)
    def _(q):
        halo_wait(q, 4 * q + 3, 4)
        steps(4 * q - 1, 4, 4 * q - 2, 4, 4 * q - 3, 4)

        @pl.when(q == 2)
        def _():
            merge(5, 0)
            merge(3, 1)

        @pl.when(q == 3)
        def _():
            merge(6, 0)
            merge(4, 1)

        @pl.when(q == 4)
        def _():
            merge(5, 1)

        @pl.when(q == 5)
        def _():
            merge(6, 1)

    halo_wait(6, 27, 4)
    steps(23, 6, 22, 8, 21, 10)

    for copy in metas:
        copy.wait_send()
    to_after.wait_send()
    to_before.wait_send()

    for p, h in EARLY + LATE:
        to_sib(p, h).wait_send()
        to_right(p, h).wait_send()
        to_left(p, h).wait_send()

    @pl.loop(0, 8)
    def _(p):
        to_up(p, 4 * p + 3, 4).wait_send()
        to_down(p, 4 * p + 3, 4).wait_send()

    for h, x in ((8, 0), (9, 35)):
        to_up(h, x, 3).wait_send()
        to_down(h, x, 3).wait_send()


def store(phases, potentials, out_phases, out_potentials, sem):
    copies = [
        pltpu.make_async_copy(phases, out_phases, sem.at[0]),
        pltpu.make_async_copy(potentials, out_potentials, sem.at[1]),
    ]
    for copy in copies:
        copy.start()
    for copy in copies:
        copy.wait()


def shards(phases, potentials, leaving, arriving, conc, latent):
    f32, i32 = jnp.float32, jnp.int32
    smem = pl.BlockSpec(memory_space=pltpu.SMEM)
    hbm = pl.BlockSpec(memory_space=pltpu.HBM)
    vmem = pl.BlockSpec(memory_space=pltpu.VMEM)
    ext = pltpu.VMEM((6, PLANES, ROWS, 128), f32)
    block = pltpu.VMEM((8, 2, 6, 16, 128), f32)
    meta = pltpu.VMEM((8, 128), i32)
    dma = pltpu.SemaphoreType.DMA
    shapes = (phases.shape, potentials.shape)
    results = pl.pallas_call(
        kernel,
        out_shape=tuple(pltpu.VMEM(s, f32) for s in shapes),
        in_specs=[hbm, hbm, hbm, smem, hbm, hbm],
        out_specs=(vmem, vmem),
        scratch_shapes=[
            ext, ext, ext, pltpu.VMEM((256, 128), jnp.bfloat16), pltpu.VMEM((2, 4), f32),
            pltpu.SMEM((1, 1), i32), pltpu.SMEM((1, 1), i32),
            block, block, block, block, block, block, block, meta, meta, meta, meta,
            dma((2, 8)), dma((3,)), dma((3,)), dma((3,)), dma((8, 2)), dma((8, 2)),
            dma((8, 2)), dma((8, 2)), dma((8, 2)), dma((8, 2)),
            dma((10,)), dma((10,)), dma((10,)), dma((10,)), dma((2,)), dma((2,)),
        ],
        compiler_params=pltpu.CompilerParams(
            collective_id=0, has_side_effects=True, vmem_limit_bytes=60 * 2**20
        ),
        cost_estimate=pl.CostEstimate(
            flops=60_000_000, bytes_accessed=6_400_000, transcendentals=0
        ),
    )(leaving, arriving, conc.T, latent.reshape(1, 4), phases, potentials)
    return tuple(
        pl.pallas_call(
            store,
            out_shape=tuple(jax.ShapeDtypeStruct(s, f32) for s in shapes),
            in_specs=[vmem, vmem],
            compiler_params=pltpu.CompilerParams(vmem_limit_bytes=2**18),
            out_specs=(hbm, hbm),
            scratch_shapes=[dma((2,))],
        )(*results)
    )


def solution(mesh):
    field = P(None, "wide", "narrow", None)
    in_specs = (field, field, P("wide", "narrow"), P("wide", "narrow"), P(), P())
    return jax.shard_map(
        shards, mesh=mesh, in_specs=in_specs, out_specs=(field, field), check_vma=False
    )
```

```python
import functools

import jax
import jax.numpy as jnp
from jax import lax
from jax.experimental import pallas as pl
from jax.experimental.pallas import tpu as pltpu
from jax.sharding import PartitionSpec as P

MESH = pl.DeviceIdType.MESH
ROW0 = 12
ROWS = 56
PLANES = 38


MXU = 4


EARLY = ((7, 0), (7, 1), (0, 0), (0, 1), (1, 0), (1, 1), (2, 0), (3, 0))
LATE = ((2, 1), (4, 0), (3, 1), (5, 0), (4, 1), (6, 0), (5, 1), (6, 1))


def neighbour_matrix():
    row = lax.broadcasted_iota(jnp.int32, (256, 128), 0) % 128
    col = lax.broadcasted_iota(jnp.int32, (256, 128), 1)
    edge = (row == col) & ((row == 0) | (row == 127))
    near = (row - col == 1) | (col - row == 1) | edge
    return near.astype(jnp.float32).astype(jnp.bfloat16)


def constants(conc, latent):
    lane = lax.broadcasted_iota(jnp.int32, (8, 128), 1)
    theta = 4.0 * (lane.astype(jnp.float32) + 0.5) / 128.0 - 2.0
    table = conc[...]
    weight = [
        [jnp.broadcast_to(table[k : k + 1, a : a + 1], (8, 128)) for k in range(2)]
        for a in range(4)
    ]
    pull = [[1.2 * weight[a][k] for k in range(2)] for a in range(4)]
    base = [1.8 + (1.2 * latent[0, a]) * theta for a in range(4)]
    return lane == 0, lane == 127, base, weight, pull


def tile_step(get, along, first, last, base, weight, pull):
    cen = [get(c, 0, 0) for c in range(6)]
    near = []
    for c in range(6):
        f = cen[c]
        if c < MXU:
            z = along(c)
        else:
            zp = jnp.where(last, f, pltpu.roll(f, 127, 1))
            zm = jnp.where(first, f, pltpu.roll(f, 1, 1))
            z = zp + zm
        near.append(((get(c, 1, 0) + get(c, -1, 0)) + (get(c, 0, 1) + get(c, 0, -1))) + z)
    rate = []
    for a in range(4):
        p = cen[a]
        q = p - p * p
        e = pull[a][0] * cen[4] + pull[a][1] * cen[5] + (base[a] - 3.6 * p)
        rate.append((0.1 * near[a] - 0.6 * p) - q * e)
    mean = 0.25 * ((rate[0] + rate[1]) + (rate[2] + rate[3]))
    change = [r - mean for r in rate]
    out = [cen[a] + change[a] for a in range(4)]
    for k in range(2):
        source = (weight[0][k] * change[0] + weight[1][k] * change[1]) + (
            weight[2][k] * change[2] + weight[3][k] * change[3]
        )
        out.append((0.4 * cen[4 + k] + 0.1 * near[4 + k]) - source)
    return out


def kernel(
    leaving_in, arriving_in, conc, latent, phases, potentials, out_phases, out_potentials,
    A, B, C, NEAR, CONC, leaving, arriving, PK, TO_SIB, SIB, SR, SL, RR, RL, META, META_SIB, META_R, META_L,
    in_sem, small_sem, meta_send, meta_recv, sib_send, sib_recv,
    r_send, r_recv, l_send, l_recv, up_send, up_recv, dn_send, dn_recv, x_send, x_recv,
):
    w, n = lax.axis_index("wide"), lax.axis_index("narrow")
    columns, rows = lax.axis_size("wide"), lax.axis_size("narrow")
    core = w % 2
    chip = w // 2
    sib = w + 1 - 2 * core
    right, left = (w + 2) % columns, (w + columns - 2) % columns
    after, before = (w + 1) % columns, (w + columns - 1) % columns
    up, down = (n + 1) % rows, (n + rows - 1) % rows

    def inputs(p):
        x = pl.ds(4 * p, 4)
        to = pl.ds(4 * p + 3, 4)
        rr = pl.ds(ROW0, 32)
        return (
            pltpu.make_async_copy(phases.at[:, x], A.at[0:4, to, rr], in_sem.at[0, p]),
            pltpu.make_async_copy(potentials.at[:, x], A.at[4:6, to, rr], in_sem.at[1, p]),
        )

    small = [
        pltpu.make_async_copy(src, dst, small_sem.at[i])
        for i, (src, dst) in enumerate(
            ((leaving_in, leaving), (arriving_in, arriving), (conc, CONC))
        )
    ]
    for copy in small:
        copy.start()
    @pl.loop(0, 8)
    def _(i):
        for copy in inputs((i + 7) % 8):
            copy.start()

    barrier = pltpu.get_barrier_semaphore()
    for device in ((right, n), (left, n), (after, n), (before, n), (w, up), (w, down)):
        pl.semaphore_signal(barrier, inc=1, device_id=device, device_id_type=MESH)

    for copy in small:
        copy.wait()
    slot = leaving[0, 0]
    source = arriving[0, 0]
    META[...] = jnp.full((8, 128), source, jnp.int32)
    lane = lax.broadcasted_iota(jnp.int32, (8, 128), 1)
    group = lane // 32

    def remote(src, dst, send, recv, device):
        return pltpu.make_async_remote_copy(
            src_ref=src, dst_ref=dst, send_sem=send, recv_sem=recv,
            device_id=device, device_id_type=MESH,
        )

    metas = (
        remote(META, META_SIB, meta_send.at[0], meta_recv.at[0], (sib, n)),
        remote(META, META_R, meta_send.at[1], meta_recv.at[1], (left, n)),
        remote(META, META_L, meta_send.at[2], meta_recv.at[2], (right, n)),
    )

    def to_sib(p, h):
        src = TO_SIB if (p, h) in EARLY else PK
        return remote(src.at[p, h], SIB.at[p, h], sib_send.at[p, h], sib_recv.at[p, h], (sib, n))

    def to_right(p, h):
        src = PK if (p, h) in EARLY else SR
        return remote(src.at[p, h], RL.at[p, h], r_send.at[p, h], r_recv.at[p, h], (right, n))

    def to_left(p, h):
        src = PK if (p, h) in EARLY else SL
        return remote(src.at[p, h], RR.at[p, h], l_send.at[p, h], l_recv.at[p, h], (left, n))

    def to_up(h, x, count):
        xs = pl.ds(x, count)
        return remote(
            A.at[:, xs, pl.ds(ROW0 + 29, 3)], A.at[:, xs, pl.ds(ROW0 - 3, 3)],
            up_send.at[h], up_recv.at[h], (w, up),
        )

    def to_down(h, x, count):
        xs = pl.ds(x, count)
        return remote(
            A.at[:, xs, pl.ds(ROW0, 3)], A.at[:, xs, pl.ds(ROW0 + 32, 3)],
            dn_send.at[h], dn_recv.at[h], (w, down),
        )

    def to_side(side):
        r = pl.ds(ROW0 - 3, 38)
        return remote(
            A.at[:, pl.ds(32 - 29 * side, 3), r], A.at[:, pl.ds(35 * side, 3), r],
            x_send.at[side], x_recv.at[side], (after + side * (before - after), n),
        )

    tiles_of = ((0, 3), (1, 2))

    def pack(p):
        for copy in inputs(p):
            copy.wait()
        shifts = [(32 * g + 128 - 32 * slot) % 128 for g in range(4)]

        for c in range(6):
            for h in range(2):
                for k, t in enumerate(tiles_of[h]):
                    r = pl.ds(ROW0 + 8 * t, 8)
                    v = [pltpu.roll(A[c, 4 * p + 3 + g, r, :], shifts[g], 1) for g in range(4)]
                    low = jnp.where(group == 0, v[0], v[1])
                    high = jnp.where(group == 2, v[2], v[3])
                    PK[p, h, c, pl.ds(8 * k, 8), :] = jnp.where(group < 2, low, high)

    def send(p, h):
        to_right(p, h).start()
        to_left(p, h).start()

    from_col = jnp.full((8, 128), source, jnp.int32)
    from_own, from_left, from_right = from_col == w, from_col == left, from_col == right
    from_sib = from_col == sib
    from_left_chip = from_left | (from_col == (sib + columns - 2) % columns)
    target = group == jnp.full((8, 128), slot, jnp.int32)

    def forward(p, h):
        to_right(p, h).wait_recv()
        to_left(p, h).wait_recv()
        want = META_SIB[...]
        own, from_l = want == w, want == left

        for c in range(6):
            for k in range(2):
                r = pl.ds(8 * k, 8)
                v = jnp.where(from_l, RL[p, h, c, r, :], RR[p, h, c, r, :])
                TO_SIB[p, h, c, r, :] = jnp.where(own, PK[p, h, c, r, :], v)

        to_sib(p, h).start()

    def route(p, h):
        to_sib(p, h).wait_recv()
        go_right, go_left = META_R[...] == sib, META_L[...] == sib
        for c in range(6):
            for k in range(2):
                r = pl.ds(8 * k, 8)
                own, other = PK[p, h, c, r, :], SIB[p, h, c, r, :]
                SR[p, h, c, r, :] = jnp.where(go_right, other, own)
                SL[p, h, c, r, :] = jnp.where(go_left, other, own)
        send(p, h)

    def merge(p, h):
        if (p, h) in EARLY:
            to_sib(p, h).wait_recv()
        else:
            to_right(p, h).wait_recv()
            to_left(p, h).wait_recv()
        shifts = [(128 + 32 * slot - 32 * g) % 128 for g in range(4)]

        for c in range(6):
            for k, t in enumerate(tiles_of[h]):
                r = pl.ds(8 * k, 8)
                if (p, h) in EARLY:
                    v = jnp.where(from_left, RL[p, h, c, r, :], SIB[p, h, c, r, :])
                    v = jnp.where(from_right, RR[p, h, c, r, :], v)
                else:
                    v = jnp.where(from_left_chip, RL[p, h, c, r, :], RR[p, h, c, r, :])
                    v = jnp.where(from_sib, SIB[p, h, c, r, :], v)
                v = jnp.where(from_own, PK[p, h, c, r, :], v)
                for g in range(4):
                    x, rr = 4 * p + 3 + g, pl.ds(ROW0 + 8 * t, 8)
                    A[c, x, rr, :] = jnp.where(target, pltpu.roll(v, shifts[g], 1), A[c, x, rr, :])

        if h == 0:
            to_up(p, 4 * p + 3, 4).start()
            to_down(p, 4 * p + 3, 4).start()

    pack(7)
    pl.semaphore_wait(barrier, 6)
    send(7, 0)
    send(7, 1)
    for copy in metas:
        copy.start()
    for p, h in EARLY[2:]:
        if h == 0:
            pack(p)
        send(p, h)
    pl.loop(4, 7)(pack)
    for p, h in LATE:
        to_sib(p, h).start()
    NEAR[...] = neighbour_matrix()
    for copy in metas:
        copy.wait_recv()

    consts = constants(CONC, latent)

    def update(src, store, x0, planes, tiles, row0):
        rows = 8 * tiles
        f = jnp.concatenate(
            [src[c, x0 + k, pl.ds(row0, rows), :] for k in range(planes) for c in range(MXU)], 0
        )
        high = f.astype(jnp.bfloat16)
        low = (f - high.astype(jnp.float32)).astype(jnp.bfloat16)
        sums = jnp.dot(
            jnp.concatenate([high, low], 1), NEAR[...], preferred_element_type=jnp.float32
        )
        for k in range(planes):
            x = x0 + k
            for t in range(tiles):
                i = row0 + 8 * t

                def get(c, dx, dy):
                    return src[c, x + dx, pl.ds(i + dy, 8), :]

                def along(c):
                    at = (k * MXU + c) * rows + 8 * t
                    return sums[at : at + 8]

                store(x, i, tile_step(get, along, *consts))

    def into(dst):
        def store(x, i, out):
            for c in range(6):
                dst[c, x, pl.ds(i, 8), :] = out[c]

        return store

    def result(x, i, out):
        for c in range(4):
            out_phases[c, x - 3, pl.ds(i - ROW0, 8), :] = out[c]
        for c in range(2):
            out_potentials[c, x - 3, pl.ds(i - ROW0, 8), :] = out[4 + c]

    def steps(a, na, b, nb, c, nc):
        update(A, into(B), a + 3, na, 5, 8)
        update(B, into(C), b + 3, nb, 5, 8)
        update(C, result, c + 3, nc, 4, ROW0)

    def halo_wait(h, x, count):
        to_up(h, x, count).wait_recv()
        to_down(h, x, count).wait_recv()

    forward(7, 0)
    forward(7, 1)
    for p, h in LATE:
        route(p, h)
    forward(0, 0)
    merge(7, 0)
    merge(7, 1)
    forward(0, 1)
    merge(0, 0)
    forward(1, 0)
    merge(0, 1)
    merge(1, 0)
    forward(1, 1)
    forward(2, 0)
    merge(1, 1)
    merge(2, 0)
    forward(3, 0)
    halo_wait(7, 31, 4)
    to_side(0).start()
    halo_wait(0, 3, 4)
    to_side(1).start()
    halo_wait(1, 7, 4)
    steps(1, 6, 2, 4, 3, 2)
    merge(3, 0)
    merge(2, 1)

    @pl.loop(2, 8)
    def _(q):
        @pl.when(q < 7)
        def _():
            halo_wait(q, 4 * q + 3, 4)

        steps(4 * q - 1, 4, 4 * q - 2, 4, 4 * q - 3, 4)

        @pl.when(q == 2)
        def _():
            merge(4, 0)
            merge(3, 1)

        @pl.when(q == 3)
        def _():
            merge(5, 0)
            merge(4, 1)

        @pl.when(q == 4)
        def _():
            merge(6, 0)
            merge(5, 1)

        @pl.when(q == 5)
        def _():
            merge(6, 1)

    @pl.loop(0, 2)
    def _(t):
        side = core * t + (1 - core) * (1 - t)
        to_side(side).wait_recv()
        steps(33 * side - 2, 3, 31 * side - 1, 3, 29 * side, 3)

    for copy in metas:
        copy.wait_send()
    to_side(0).wait_send()
    to_side(1).wait_send()

    for p, h in EARLY + LATE:
        to_sib(p, h).wait_send()
        to_right(p, h).wait_send()
        to_left(p, h).wait_send()

    @pl.loop(0, 8)
    def _(p):
        to_up(p, 4 * p + 3, 4).wait_send()
        to_down(p, 4 * p + 3, 4).wait_send()


def store(phases, potentials, out_phases, out_potentials, sem):
    copies = [
        pltpu.make_async_copy(phases, out_phases, sem.at[0]),
        pltpu.make_async_copy(potentials, out_potentials, sem.at[1]),
    ]
    for copy in copies:
        copy.start()
    for copy in copies:
        copy.wait()


def shards(phases, potentials, leaving, arriving, conc, latent):
    f32, i32 = jnp.float32, jnp.int32
    smem = pl.BlockSpec(memory_space=pltpu.SMEM)
    hbm = pl.BlockSpec(memory_space=pltpu.HBM)
    vmem = pl.BlockSpec(memory_space=pltpu.VMEM)
    ext = pltpu.VMEM((6, PLANES, ROWS, 128), f32)
    block = pltpu.VMEM((8, 2, 6, 16, 128), f32)
    meta = pltpu.VMEM((8, 128), i32)
    dma = pltpu.SemaphoreType.DMA
    shapes = (phases.shape, potentials.shape)
    results = pl.pallas_call(
        kernel,
        out_shape=tuple(pltpu.VMEM(s, f32) for s in shapes),
        in_specs=[hbm, hbm, hbm, smem, hbm, hbm],
        out_specs=(vmem, vmem),
        scratch_shapes=[
            ext, ext, ext, pltpu.VMEM((256, 128), jnp.bfloat16), pltpu.VMEM((2, 4), f32),
            pltpu.SMEM((1, 1), i32), pltpu.SMEM((1, 1), i32),
            block, block, block, block, block, block, block, meta, meta, meta, meta,
            dma((2, 8)), dma((3,)), dma((3,)), dma((3,)), dma((8, 2)), dma((8, 2)),
            dma((8, 2)), dma((8, 2)), dma((8, 2)), dma((8, 2)),
            dma((8,)), dma((8,)), dma((8,)), dma((8,)), dma((2,)), dma((2,)),
        ],
        compiler_params=pltpu.CompilerParams(
            collective_id=0, has_side_effects=True, vmem_limit_bytes=60 * 2**20
        ),
        cost_estimate=pl.CostEstimate(
            flops=60_000_000, bytes_accessed=6_400_000, transcendentals=0
        ),
    )(leaving, arriving, conc.T, latent.reshape(1, 4), phases, potentials)
    return tuple(
        pl.pallas_call(
            store,
            out_shape=tuple(jax.ShapeDtypeStruct(s, f32) for s in shapes),
            in_specs=[vmem, vmem],
            compiler_params=pltpu.CompilerParams(vmem_limit_bytes=2**18),
            out_specs=(hbm, hbm),
            scratch_shapes=[dma((2,))],
        )(*results)
    )


def solution(mesh):
    field = P(None, "wide", "narrow", None)
    in_specs = (field, field, P("wide", "narrow"), P("wide", "narrow"), P(), P())
    return jax.shard_map(
        shards, mesh=mesh, in_specs=in_specs, out_specs=(field, field), check_vma=False
    )
```

```python
import functools

import jax
import jax.numpy as jnp
from jax import lax
from jax.experimental import pallas as pl
from jax.experimental.pallas import tpu as pltpu
from jax.sharding import PartitionSpec as P

MESH = pl.DeviceIdType.MESH
ROW0 = 12
ROWS = 56
PLANES = 38


MXU = 4


EARLY = ((7, 0), (7, 1), (0, 0), (0, 1), (1, 0), (1, 1), (2, 0), (3, 0))
LATE = ((2, 1), (4, 0), (3, 1), (5, 0), (4, 1), (6, 0), (5, 1), (6, 1))


def neighbour_matrix():
    row = lax.broadcasted_iota(jnp.int32, (256, 128), 0) % 128
    col = lax.broadcasted_iota(jnp.int32, (256, 128), 1)
    edge = (row == col) & ((row == 0) | (row == 127))
    near = (row - col == 1) | (col - row == 1) | edge
    return near.astype(jnp.float32).astype(jnp.bfloat16)


def constants(conc, latent):
    lane = lax.broadcasted_iota(jnp.int32, (8, 128), 1)
    theta = 4.0 * (lane.astype(jnp.float32) + 0.5) / 128.0 - 2.0
    table = conc[...]
    weight = [
        [jnp.broadcast_to(table[k : k + 1, a : a + 1], (8, 128)) for k in range(2)]
        for a in range(4)
    ]
    pull = [[1.2 * weight[a][k] for k in range(2)] for a in range(4)]
    base = [1.8 + (1.2 * latent[0, a]) * theta for a in range(4)]
    return lane == 0, lane == 127, base, weight, pull


def tile_step(get, along, first, last, base, weight, pull):
    cen = [get(c, 0, 0) for c in range(6)]
    near = []
    for c in range(6):
        f = cen[c]
        if c < MXU:
            z = along(c)
        else:
            zp = jnp.where(last, f, pltpu.roll(f, 127, 1))
            zm = jnp.where(first, f, pltpu.roll(f, 1, 1))
            z = zp + zm
        near.append(((get(c, 1, 0) + get(c, -1, 0)) + (get(c, 0, 1) + get(c, 0, -1))) + z)
    rate = []
    for a in range(4):
        p = cen[a]
        q = p - p * p
        e = pull[a][0] * cen[4] + pull[a][1] * cen[5] + (base[a] - 3.6 * p)
        rate.append((0.1 * near[a] - 0.6 * p) - q * e)
    mean = 0.25 * ((rate[0] + rate[1]) + (rate[2] + rate[3]))
    change = [r - mean for r in rate]
    out = [cen[a] + change[a] for a in range(4)]
    for k in range(2):
        source = (weight[0][k] * change[0] + weight[1][k] * change[1]) + (
            weight[2][k] * change[2] + weight[3][k] * change[3]
        )
        out.append((0.4 * cen[4 + k] + 0.1 * near[4 + k]) - source)
    return out


def kernel(
    leaving_in, arriving_in, conc, latent, phases, potentials, out_phases, out_potentials,
    A, B, C, NEAR, CONC, leaving, arriving, PK, TO_SIB, SIB, SR, SL, RR, RL, META, META_SIB, META_R, META_L,
    in_sem, small_sem, meta_send, meta_recv, sib_send, sib_recv,
    r_send, r_recv, l_send, l_recv, up_send, up_recv, dn_send, dn_recv, x_send, x_recv,
):
    w, n = lax.axis_index("wide"), lax.axis_index("narrow")
    columns, rows = lax.axis_size("wide"), lax.axis_size("narrow")
    core = w % 2
    chip = w // 2
    sib = w + 1 - 2 * core
    right, left = (w + 2) % columns, (w + columns - 2) % columns
    after, before = (w + 1) % columns, (w + columns - 1) % columns
    up, down = (n + 1) % rows, (n + rows - 1) % rows

    def inputs(p):
        x = pl.ds(4 * p, 4)
        to = pl.ds(4 * p + 3, 4)
        rr = pl.ds(ROW0, 32)
        return (
            pltpu.make_async_copy(phases.at[:, x], A.at[0:4, to, rr], in_sem.at[0, p]),
            pltpu.make_async_copy(potentials.at[:, x], A.at[4:6, to, rr], in_sem.at[1, p]),
        )

    small = [
        pltpu.make_async_copy(src, dst, small_sem.at[i])
        for i, (src, dst) in enumerate(
            ((leaving_in, leaving), (arriving_in, arriving), (conc, CONC))
        )
    ]
    for copy in small:
        copy.start()
    @pl.loop(0, 8)
    def _(i):
        for copy in inputs((i + 7) % 8):
            copy.start()

    barrier = pltpu.get_barrier_semaphore()
    for device in ((right, n), (left, n), (after, n), (before, n), (w, up), (w, down)):
        pl.semaphore_signal(barrier, inc=1, device_id=device, device_id_type=MESH)

    for copy in small:
        copy.wait()
    slot = leaving[0, 0]
    source = arriving[0, 0]
    META[...] = jnp.full((8, 128), source, jnp.int32)
    lane = lax.broadcasted_iota(jnp.int32, (8, 128), 1)
    group = lane // 32

    def remote(src, dst, send, recv, device):
        return pltpu.make_async_remote_copy(
            src_ref=src, dst_ref=dst, send_sem=send, recv_sem=recv,
            device_id=device, device_id_type=MESH,
        )

    metas = (
        remote(META, META_SIB, meta_send.at[0], meta_recv.at[0], (sib, n)),
        remote(META, META_R, meta_send.at[1], meta_recv.at[1], (left, n)),
        remote(META, META_L, meta_send.at[2], meta_recv.at[2], (right, n)),
    )

    def to_sib(p, h):
        src = TO_SIB if (p, h) in EARLY else PK
        return remote(src.at[p, h], SIB.at[p, h], sib_send.at[p, h], sib_recv.at[p, h], (sib, n))

    def to_right(p, h):
        src = PK if (p, h) in EARLY else SR
        return remote(src.at[p, h], RL.at[p, h], r_send.at[p, h], r_recv.at[p, h], (right, n))

    def to_left(p, h):
        src = PK if (p, h) in EARLY else SL
        return remote(src.at[p, h], RR.at[p, h], l_send.at[p, h], l_recv.at[p, h], (left, n))

    def to_up(h, x, count):
        xs = pl.ds(x, count)
        return remote(
            A.at[:, xs, pl.ds(ROW0 + 29, 3)], A.at[:, xs, pl.ds(ROW0 - 3, 3)],
            up_send.at[h], up_recv.at[h], (w, up),
        )

    def to_down(h, x, count):
        xs = pl.ds(x, count)
        return remote(
            A.at[:, xs, pl.ds(ROW0, 3)], A.at[:, xs, pl.ds(ROW0 + 32, 3)],
            dn_send.at[h], dn_recv.at[h], (w, down),
        )

    def to_side(side):
        r = pl.ds(ROW0 - 3, 38)
        return remote(
            A.at[:, pl.ds(32 - 29 * side, 3), r], A.at[:, pl.ds(35 * side, 3), r],
            x_send.at[side], x_recv.at[side], (after + side * (before - after), n),
        )

    tiles_of = ((0, 3), (1, 2))

    def pack(p):
        for copy in inputs(p):
            copy.wait()
        shifts = [(32 * g + 128 - 32 * slot) % 128 for g in range(4)]

        for c in range(6):
            for h in range(2):
                for k, t in enumerate(tiles_of[h]):
                    r = pl.ds(ROW0 + 8 * t, 8)
                    v = [pltpu.roll(A[c, 4 * p + 3 + g, r, :], shifts[g], 1) for g in range(4)]
                    low = jnp.where(group == 0, v[0], v[1])
                    high = jnp.where(group == 2, v[2], v[3])
                    PK[p, h, c, pl.ds(8 * k, 8), :] = jnp.where(group < 2, low, high)

    def send(p, h):
        to_right(p, h).start()
        to_left(p, h).start()

    from_col = jnp.full((8, 128), source, jnp.int32)
    from_own, from_left, from_right = from_col == w, from_col == left, from_col == right
    from_sib = from_col == sib
    from_left_chip = from_left | (from_col == (sib + columns - 2) % columns)
    target = group == jnp.full((8, 128), slot, jnp.int32)

    def forward(p, h):
        to_right(p, h).wait_recv()
        to_left(p, h).wait_recv()
        want = META_SIB[...]
        own, from_l = want == w, want == left

        for c in range(6):
            for k in range(2):
                r = pl.ds(8 * k, 8)
                v = jnp.where(from_l, RL[p, h, c, r, :], RR[p, h, c, r, :])
                TO_SIB[p, h, c, r, :] = jnp.where(own, PK[p, h, c, r, :], v)

        to_sib(p, h).start()

    def route(p, h):
        to_sib(p, h).wait_recv()
        go_right, go_left = META_R[...] == sib, META_L[...] == sib
        for c in range(6):
            for k in range(2):
                r = pl.ds(8 * k, 8)
                own, other = PK[p, h, c, r, :], SIB[p, h, c, r, :]
                SR[p, h, c, r, :] = jnp.where(go_right, other, own)
                SL[p, h, c, r, :] = jnp.where(go_left, other, own)
        send(p, h)

    def merge(p, h):
        if (p, h) in EARLY:
            to_sib(p, h).wait_recv()
        else:
            to_right(p, h).wait_recv()
            to_left(p, h).wait_recv()
        shifts = [(128 + 32 * slot - 32 * g) % 128 for g in range(4)]

        for c in range(6):
            for k, t in enumerate(tiles_of[h]):
                r = pl.ds(8 * k, 8)
                if (p, h) in EARLY:
                    v = jnp.where(from_left, RL[p, h, c, r, :], SIB[p, h, c, r, :])
                    v = jnp.where(from_right, RR[p, h, c, r, :], v)
                else:
                    v = jnp.where(from_left_chip, RL[p, h, c, r, :], RR[p, h, c, r, :])
                    v = jnp.where(from_sib, SIB[p, h, c, r, :], v)
                v = jnp.where(from_own, PK[p, h, c, r, :], v)
                for g in range(4):
                    x, rr = 4 * p + 3 + g, pl.ds(ROW0 + 8 * t, 8)
                    A[c, x, rr, :] = jnp.where(target, pltpu.roll(v, shifts[g], 1), A[c, x, rr, :])

        if h == 0:
            to_up(p, 4 * p + 3, 4).start()
            to_down(p, 4 * p + 3, 4).start()

    pack(7)
    pl.semaphore_wait(barrier, 6)
    send(7, 0)
    send(7, 1)
    for copy in metas:
        copy.start()
    for p, h in EARLY[2:]:
        if h == 0:
            pack(p)
        send(p, h)
    pl.loop(4, 7)(pack)
    for p, h in LATE:
        to_sib(p, h).start()
    NEAR[...] = neighbour_matrix()
    for copy in metas:
        copy.wait_recv()

    consts = constants(CONC, latent)

    def update(src, store, x0, planes, tiles, row0):
        rows = 8 * tiles
        f = jnp.concatenate(
            [src[c, x0 + k, pl.ds(row0, rows), :] for k in range(planes) for c in range(MXU)], 0
        )
        high = f.astype(jnp.bfloat16)
        low = (f - high.astype(jnp.float32)).astype(jnp.bfloat16)
        sums = jnp.dot(
            jnp.concatenate([high, low], 1), NEAR[...], preferred_element_type=jnp.float32
        )
        for k in range(planes):
            x = x0 + k
            for t in range(tiles):
                i = row0 + 8 * t

                def get(c, dx, dy):
                    return src[c, x + dx, pl.ds(i + dy, 8), :]

                def along(c):
                    at = (k * MXU + c) * rows + 8 * t
                    return sums[at : at + 8]

                store(x, i, tile_step(get, along, *consts))

    def into(dst):
        def store(x, i, out):
            for c in range(6):
                dst[c, x, pl.ds(i, 8), :] = out[c]

        return store

    def result(x, i, out):
        for c in range(4):
            out_phases[c, x - 3, pl.ds(i - ROW0, 8), :] = out[c]
        for c in range(2):
            out_potentials[c, x - 3, pl.ds(i - ROW0, 8), :] = out[4 + c]

    def steps(a, na, b, nb, c, nc):
        update(A, into(B), a + 3, na, 5, 8)
        update(B, into(C), b + 3, nb, 5, 8)
        update(C, result, c + 3, nc, 4, ROW0)

    def halo_wait(h, x, count):
        to_up(h, x, count).wait_recv()
        to_down(h, x, count).wait_recv()

    forward(7, 0)
    forward(7, 1)
    for p, h in LATE:
        route(p, h)
    forward(0, 0)
    merge(7, 0)
    merge(7, 1)
    forward(0, 1)
    merge(0, 0)
    forward(1, 0)
    merge(0, 1)
    merge(1, 0)
    forward(1, 1)
    forward(2, 0)
    merge(1, 1)
    merge(2, 0)
    forward(3, 0)
    halo_wait(7, 31, 4)
    to_side(0).start()
    halo_wait(0, 3, 4)
    to_side(1).start()
    merge(3, 0)
    halo_wait(1, 7, 4)
    steps(1, 6, 2, 4, 3, 2)

    @pl.loop(2, 8)
    def _(q):
        @pl.when(q == 2)
        def _():
            merge(2, 1)
            merge(4, 0)
            merge(3, 1)

        @pl.when(q == 3)
        def _():
            merge(5, 0)
            merge(4, 1)
            merge(6, 0)

        @pl.when(q == 4)
        def _():
            merge(5, 1)

        @pl.when(q == 5)
        def _():
            merge(6, 1)

        @pl.when(q < 7)
        def _():
            halo_wait(q, 4 * q + 3, 4)

        steps(4 * q - 1, 4, 4 * q - 2, 4, 4 * q - 3, 4)

    @pl.loop(0, 2)
    def _(t):
        side = core * t + (1 - core) * (1 - t)
        to_side(side).wait_recv()
        steps(33 * side - 2, 3, 31 * side - 1, 3, 29 * side, 3)

    for copy in metas:
        copy.wait_send()
    to_side(0).wait_send()
    to_side(1).wait_send()

    for p, h in EARLY + LATE:
        to_sib(p, h).wait_send()
        to_right(p, h).wait_send()
        to_left(p, h).wait_send()

    @pl.loop(0, 8)
    def _(p):
        to_up(p, 4 * p + 3, 4).wait_send()
        to_down(p, 4 * p + 3, 4).wait_send()


def store(phases, potentials, out_phases, out_potentials, sem):
    copies = [
        pltpu.make_async_copy(phases, out_phases, sem.at[0]),
        pltpu.make_async_copy(potentials, out_potentials, sem.at[1]),
    ]
    for copy in copies:
        copy.start()
    for copy in copies:
        copy.wait()


def shards(phases, potentials, leaving, arriving, conc, latent):
    f32, i32 = jnp.float32, jnp.int32
    smem = pl.BlockSpec(memory_space=pltpu.SMEM)
    hbm = pl.BlockSpec(memory_space=pltpu.HBM)
    vmem = pl.BlockSpec(memory_space=pltpu.VMEM)
    ext = pltpu.VMEM((6, PLANES, ROWS, 128), f32)
    block = pltpu.VMEM((8, 2, 6, 16, 128), f32)
    meta = pltpu.VMEM((8, 128), i32)
    dma = pltpu.SemaphoreType.DMA
    shapes = (phases.shape, potentials.shape)
    results = pl.pallas_call(
        kernel,
        out_shape=tuple(pltpu.VMEM(s, f32) for s in shapes),
        in_specs=[hbm, hbm, hbm, smem, hbm, hbm],
        out_specs=(vmem, vmem),
        scratch_shapes=[
            ext, ext, ext, pltpu.VMEM((256, 128), jnp.bfloat16), pltpu.VMEM((2, 4), f32),
            pltpu.SMEM((1, 1), i32), pltpu.SMEM((1, 1), i32),
            block, block, block, block, block, block, block, meta, meta, meta, meta,
            dma((2, 8)), dma((3,)), dma((3,)), dma((3,)), dma((8, 2)), dma((8, 2)),
            dma((8, 2)), dma((8, 2)), dma((8, 2)), dma((8, 2)),
            dma((8,)), dma((8,)), dma((8,)), dma((8,)), dma((2,)), dma((2,)),
        ],
        compiler_params=pltpu.CompilerParams(
            collective_id=0, has_side_effects=True, vmem_limit_bytes=60 * 2**20
        ),
        cost_estimate=pl.CostEstimate(
            flops=60_000_000, bytes_accessed=6_400_000, transcendentals=0
        ),
    )(leaving, arriving, conc.T, latent.reshape(1, 4), phases, potentials)
    return tuple(
        pl.pallas_call(
            store,
            out_shape=tuple(jax.ShapeDtypeStruct(s, f32) for s in shapes),
            in_specs=[vmem, vmem],
            compiler_params=pltpu.CompilerParams(vmem_limit_bytes=2**18),
            out_specs=(hbm, hbm),
            scratch_shapes=[dma((2,))],
        )(*results)
    )


def solution(mesh):
    field = P(None, "wide", "narrow", None)
    in_specs = (field, field, P("wide", "narrow"), P("wide", "narrow"), P(), P())
    return jax.shard_map(
        shards, mesh=mesh, in_specs=in_specs, out_specs=(field, field), check_vma=False
    )
```
